32 devices in a mesh: table: 8 (over y, x, core), sample: 4 (over z).
Axes of the slice: x: 2, y: 2, z: 4, core: 2. Of those that a mesh axis runs over, the one named last changes fastest.
Arguments:
- hist_ids: int32 [512, 8, 48], P(('table', 'sample')), may hold values from 0 to 2047
- hist_lens: int32 [512, 8], P(('table', 'sample')), may hold values from 1 to 48, 256 in all within a row
- table_rows: bfloat16 [16384, 256], P('table'), may hold values from -6 to 6
- imp_user: int32 [8192], P(('table', 'sample')), may hold values from 0 to 63
- item_rows: bfloat16 [8192, 256], P(('table', 'sample')), may hold values from -6 to 6
- labels: int32 [8192], P(('table', 'sample')), may hold values 0 or 1
- w_hidden: bfloat16 [512, 512], replicated, may hold values from -0.25 to 0.25
- b_hidden: float32 [512], replicated, may hold values from -3 to 3
- w_back: bfloat16 [512, 512], replicated, may hold values from -0.25 to 0.25
- w_cross: bfloat16 [512, 512], replicated, may hold values from -0.25 to 0.25
- b_cross: float32 [512], replicated, may hold values from -4 to 4
- norm_gain: float32 [512], replicated, may hold values from 0.25 to 1.75
- w_score: float32 [512], replicated, may hold values from -0.25 to 0.25
Outputs:
- pooled_user: bfloat16 [512, 256], P(('table', 'sample'))
- scores: float32 [8192], P(('table', 'sample'))
- user_grad: float32 [512, 256], P(('table', 'sample'))
- item_grad: float32 [8192, 256], P(('table', 'sample'))
The draws below stay inside these ranges and needn't reach their ends.
Inputs may be any that keep to these rules, and one draw needn't show every extreme that they name: `hist_lens`: each user's live ids over all shards number exactly 256; some user has 48 live ids in one shard. `imp_user`: an impression names one of the 64 users held by the devices of its own table index.
All inputs are finite; a program needn't handle non-finite values. No bound on the sum of `labels` on one device may be relied on, other than what follows from the above.
Results may differ from the reference program's by a relative error of at most 0.02.
Values may be sent and summed in bfloat16 or wider, within the bound.
A program may use at most 64 MiB of HBM per device.

```python
import math
import jax
import jax.numpy as jnp
import numpy as np
from jax import lax

E = 256
FF = 512
CAP = 48
U_DEV = 16
IMP_DEV = 256
ROWS_DEV = 2048
HIST = 256
USERS = 512
IMPS = 8192
ROWS = 16384
N_TABLE = 8
N_SAMPLE = 4
DEVICES = 32


def touch_ends(result, own_key, low, high):
    spot = [jax.random.randint(jax.random.fold_in(own_key, axis), (), 0, length) for axis, length in enumerate(result.shape)]
    main_axis = result.shape.index(max(result.shape))
    beside = spot[:main_axis] + [(spot[main_axis] + 1) % result.shape[main_axis]] + spot[main_axis + 1:]
    return result.at[tuple(spot)].set(low).at[tuple(beside)].set(high)


def level_of(key, dims, cuts, least, largest):
    def one(dim, blocks):
        steps = jax.random.uniform(jax.random.fold_in(jax.random.fold_in(key, 6), dim), (blocks,), jnp.float32, least / len(cuts), largest / len(cuts))
        return jnp.repeat(jnp.exp(steps), dims[dim] // blocks).reshape((-1,) + (1,) * (len(dims) - dim - 1))

    factor_of = one(*cuts[0])
    for cut in cuts[1:]:
        factor_of = factor_of * one(*cut)
    return factor_of


def rank_bounds(number_of, skew):
    portions = [(1 << 20) // math.isqrt(grade ** skew) + 1 for grade in range(1, number_of + 1)]
    width = 1 + sum(portions) // (1 << 30)
    return np.cumsum(np.array([max(1, weight // width) for weight in portions]))


def skewed_ids(own_key, extent, number_of, lean):
    table = rank_bounds(number_of, lean)
    ticket = jax.random.randint(jax.random.fold_in(own_key, 1), extent, 0, int(table[number_of - 1]))
    rank = jnp.searchsorted(jnp.asarray(table, jnp.int32), ticket, side="right")
    return jax.random.permutation(jax.random.fold_in(own_key, 2), number_of)[rank].astype(jnp.int32)


def split_up(count, total, limit, lean):
    weights = [(1 << 20) // math.isqrt(standing ** lean) + 1 for standing in range(2, count + 1)]
    rest, holding = total - limit - (count - 1), [1] * (count - 1)
    while rest > 0:
        movable = [i for i in range(count - 1) if holding[i] < limit]
        pool, budget = sum([weights[i] for i in movable]), rest
        for i in movable:
            extra = min(limit - holding[i], max(1, budget * weights[i] // pool), rest)
            holding[i] = holding[i] + extra
            rest = rest - extra
    return np.array([limit] + holding)


def ragged_sizes(own_key, amount, total, limit, skew):
    if amount == 2:
        one = jax.random.randint(own_key, (), max(1, total - limit), min(limit, total - 1) + 1)
        return jnp.stack([one, total - one])
    lengths = jnp.asarray(split_up(amount, total, limit, skew), jnp.int32)
    twos = (amount - 1) // 2
    donor, sink = lengths[1:1 + 2 * twos:2], lengths[2:2 + 2 * twos:2]
    room = jnp.minimum(donor - 1, limit - sink)
    moved = jax.random.randint(jax.random.fold_in(own_key, 1), (twos,), 0, 1 << 20) % (room + 1)
    lengths = lengths.at[1:1 + 2 * twos:2].set(donor - moved).at[2:2 + 2 * twos:2].set(sink + moved)
    return lengths[jax.random.permutation(jax.random.fold_in(own_key, 2), amount)]


def noise(stream_key, shape, spread, limit, split=(), held_as=jnp.bfloat16):
    entries = spread * jax.random.normal(stream_key, shape, jnp.float32)
    if split:
        entries = entries * level_of(stream_key, shape, split, -0.22, 0.18)
    return jnp.clip(entries, -limit, limit).astype(held_as)


def setup_inputs(seed: int = 0) -> dict:
    splits = jax.random.split(jax.random.key(seed), 14)
    hist_ids = touch_ends(jax.random.randint(splits[0], (USERS, N_TABLE, CAP), 0, ROWS_DEV), jax.random.fold_in(splits[0], 1), 0, ROWS_DEV - 1).astype(jnp.int32)
    hist_lens = jax.vmap(lambda own: ragged_sizes(own, N_TABLE, HIST, CAP, 2))(jax.random.split(splits[1], USERS)).reshape((USERS, N_TABLE)).astype(jnp.int32)
    table_rows = noise(splits[2], (ROWS, E), 1.0, 6.0, ((0, 8),))
    imp_user = touch_ends(skewed_ids(splits[3], (IMPS,), U_DEV * N_SAMPLE, 2), jax.random.fold_in(splits[3], 3), 0, (U_DEV * N_SAMPLE) - 1).astype(jnp.int32)
    item_rows = noise(splits[4], (IMPS, E), 1.0, 6.0, ((0, 32),))
    labels = touch_ends((jax.random.randint(splits[5], (IMPS,), 0, 4) < 1).astype(jnp.int32), jax.random.fold_in(splits[5], 1), 0, 1)
    w_hidden = noise(splits[6], (2 * E, FF), (2 * E) ** -0.5, 0.25)
    b_hidden = noise(splits[7], (FF,), 0.5, 3.0, (), jnp.float32)
    w_back = noise(splits[8], (FF, 2 * E), FF ** -0.5, 0.25)
    w_cross = noise(splits[9], (2 * E, 2 * E), (2 * E) ** -0.5, 0.25)
    b_cross = noise(splits[10], (2 * E,), 1.0, 4.0, (), jnp.float32)
    norm_gain = jnp.clip(1.0 + 0.15 * jax.random.normal(splits[11], (2 * E,), jnp.float32), 0.25, 1.75)
    w_score = noise(splits[12], (2 * E,), (2 * E) ** -0.5, 0.25, (), jnp.float32)
    return dict(hist_ids=hist_ids, hist_lens=hist_lens, table_rows=table_rows, imp_user=imp_user, item_rows=item_rows, labels=labels, w_hidden=w_hidden, b_hidden=b_hidden, w_back=w_back, w_cross=w_cross, b_cross=b_cross, norm_gain=norm_gain, w_score=w_score)


def forward(user_in, item_in, w_hidden, b_hidden, w_back, w_cross, b_cross, norm_gain, w_score):
    joined = jnp.concatenate([user_in, item_in], axis=1).astype(jnp.bfloat16)
    hidden = jax.nn.gelu(jnp.dot(joined, w_hidden, preferred_element_type=jnp.float32) + b_hidden).astype(jnp.bfloat16)
    mlp_out = jnp.dot(hidden, w_back, preferred_element_type=jnp.float32)
    lifted = joined.astype(jnp.float32)
    crossed = lifted * (jnp.dot(joined, w_cross, preferred_element_type=jnp.float32) + b_cross)
    summed = lifted + mlp_out + crossed
    row_mean = lax.optimization_barrier(jnp.mean(summed, axis=1, keepdims=True))
    centred = summed - row_mean
    row_var = lax.optimization_barrier(jnp.mean(centred * centred, axis=1, keepdims=True))
    normed = centred * lax.rsqrt(row_var + 1e-05) * norm_gain
    return jnp.dot(normed, w_score, precision=lax.Precision.HIGHEST)

def reference(hist_ids, hist_lens, table_rows, imp_user, item_rows, labels, w_hidden, b_hidden, w_back, w_cross, b_cross, norm_gain, w_score):
    owner_base = jnp.arange(N_TABLE, dtype=jnp.int32) * ROWS_DEV

    def pool_block(pair):
        block_ids, block_lens = pair
        gathered = jnp.take(table_rows, block_ids + owner_base[None, :, None], axis=0)
        live_slots = lax.broadcasted_iota(jnp.int32, block_ids.shape, 2) < block_lens[:, :, None]
        return lax.optimization_barrier(jnp.sum(jnp.where(live_slots[..., None], gathered.astype(jnp.float32), jnp.float32(0.0)), axis=(1, 2)))
    pooled_sum = lax.map(pool_block, (hist_ids.reshape(DEVICES, U_DEV, N_TABLE, CAP), hist_lens.reshape(DEVICES, U_DEV, N_TABLE)))
    pooled_sum = pooled_sum.reshape(USERS, E)
    pooled_user = (pooled_sum * float(HIST) ** (-0.5)).astype(jnp.bfloat16)
    group_rows = IMP_DEV * N_SAMPLE
    offsets = jnp.arange(IMPS, dtype=jnp.int32) // group_rows * (U_DEV * N_SAMPLE)
    global_user = (imp_user + offsets).astype(jnp.int32)
    user_feat = jnp.take(pooled_user, global_user, axis=0)

    def group_step(pair):
        user_block, item_block, label_block = pair

        def score_of(user_in, item_in):
            return forward(user_in, item_in, w_hidden, b_hidden, w_back, w_cross, b_cross, norm_gain, w_score)
        block_scores, pullback = jax.vjp(score_of, user_block.astype(jnp.float32), item_block.astype(jnp.float32))
        score_grad = jax.nn.sigmoid(block_scores) - label_block.astype(jnp.float32)
        user_part, item_part = pullback(score_grad)
        return (block_scores, user_part, item_part)
    groups_count = IMPS // group_rows
    scores, user_part, item_grad = lax.map(group_step, (user_feat.reshape(groups_count, group_rows, E), item_rows.reshape(groups_count, group_rows, E), labels.reshape(groups_count, group_rows)))
    scores = scores.reshape(IMPS)
    user_part = user_part.reshape(IMPS, E)
    item_grad = item_grad.reshape(IMPS, E)
    user_grad = jax.ops.segment_sum(user_part, global_user, num_segments=USERS)
    return (pooled_user, scores, user_grad, item_grad)
```

```python
import functools

import jax
import jax.numpy as jnp
from jax import lax
from jax.experimental import pallas as pl
from jax.experimental.pallas import tpu as pltpu
from jax.sharding import PartitionSpec as P

MESH = pl.DeviceIdType.MESH
F32 = jnp.float32
BF16 = jnp.bfloat16
LANES = 128
GELU_A = 0.7978845608028654
GELU_B = 0.044715


def dot_nn(a, b):
    return lax.dot_general(a, b, (((1,), (0,)), ((), ())), preferred_element_type=F32)


def dot_nt(a, b):
    return lax.dot_general(a, b, (((1,), (1,)), ((), ())), preferred_element_type=F32)


def to_column(row, width):
    return jnp.transpose(jnp.broadcast_to(row, (width, row.shape[1])))


def each(count, body):
    if count <= 8:
        for i in range(count):
            body(i)
    else:
        lax.fori_loop(0, count, lambda i, c: (body(i), c)[1], 0)


def kernel(
    scale,
    ids_ref,
    lens_ref,
    table_hbm,
    imp_ref,
    item_hbm,
    label_ref,
    wh_hbm,
    bh_ref,
    wb_hbm,
    wc_hbm,
    bc_ref,
    gain_ref,
    ws_ref,
    pooled_out,
    scores_out,
    ugrad_out,
    igrad_hbm,
    table_v,
    item_v,
    wh_v,
    wb_v,
    wc_v,
    msg,
    got,
    counts,
    part_send,
    part_recv,
    pool_all,
    grad_send,
    grad_recv,
    igrad_v,
    load_sem,
    ids_ssem,
    ids_rsem,
    part_ssem,
    part_rsem,
    pool_ssem,
    pool_rsem,
    grad_ssem,
    grad_rsem,
):
    tables, chunks = msg.shape[0], msg.shape[1]
    samples = pool_all.shape[0]
    users, _, slots = ids_ref.shape
    width = table_v.shape[1]
    n_hi = table_v.shape[0] // LANES
    imps = item_v.shape[0]
    group = samples * users
    t = lax.axis_index("table")
    s = lax.axis_index("sample")

    def table_peer(d):
        return lax.rem(t + d, tables)

    def sample_peer(d):
        return lax.rem(s + d, samples)

    barrier = pltpu.get_barrier_semaphore()

    def greet_table(i):
        pl.semaphore_signal(barrier, inc=1, device_id=(table_peer(i + 1), s), device_id_type=MESH)

    def greet_sample(i):
        pl.semaphore_signal(barrier, inc=1, device_id=(t, sample_peer(i + 1)), device_id_type=MESH)

    each(tables - 1, greet_table)
    each(samples - 1, greet_sample)

    loads = [
        pltpu.make_async_copy(src, dst, load_sem.at[i])
        for i, (src, dst) in enumerate(
            [
                (table_hbm, table_v),
                (item_hbm, item_v),
                (wh_hbm, wh_v),
                (wc_hbm, wc_v),
                (wb_hbm, wb_v),
            ]
        )
    ]
    for load in loads:
        load.start()

    eye = lax.broadcasted_iota(jnp.int32, (tables, tables), 0) == lax.broadcasted_iota(
        jnp.int32, (tables, tables), 1
    )
    slot_iota = lax.broadcasted_iota(jnp.int32, (tables, slots), 1)
    pieces = []
    for u in range(users):
        lens_u = jnp.broadcast_to(lens_ref[u : u + 1, :], (tables, tables))
        len_col = jnp.sum(jnp.where(eye, lens_u, 0), axis=1, keepdims=True)
        pieces.append(jnp.where(slot_iota < len_col, ids_ref[u], -1))
    packed = jnp.concatenate(pieces, axis=1)
    for c in range(users * slots // LANES):
        msg[:, c, :] = packed[:, c * LANES : (c + 1) * LANES]
    for c in range(users * slots // LANES, chunks):
        msg[:, c, :] = jnp.full((tables, LANES), -1, jnp.int32)

    pl.semaphore_wait(barrier, tables - 1 + samples - 1)

    def ids_copy(dst_table, owner, src_table):
        return pltpu.make_async_remote_copy(
            src_ref=msg.at[src_table],
            dst_ref=got.at[owner],
            send_sem=ids_ssem.at[src_table],
            recv_sem=ids_rsem.at[owner],
            device_id=(dst_table, s),
            device_id_type=MESH,
        )

    def send_ids(i):
        peer = table_peer(i + 1)
        ids_copy(peer, t, peer).start()

    each(tables - 1, send_ids)
    got[t] = msg[t]

    imp_row = imp_ref[...].astype(F32)
    imp_col = to_column(imp_row, LANES)[:, :1]
    picks = jnp.where(
        imp_col == lax.broadcasted_iota(jnp.int32, (imps, group), 1).astype(F32), 1.0, 0.0
    ).astype(BF16)
    picks_t = jnp.where(
        imp_ref[...] == lax.broadcasted_iota(jnp.int32, (group, imps), 0), 1.0, 0.0
    ).astype(BF16)
    label_col = to_column(label_ref[...].astype(F32), LANES)[:, :1]
    v_row = gain_ref[...] * ws_ref[...]
    v_centred = v_row - jnp.mean(v_row, axis=1, keepdims=True)

    position = (
        lax.broadcasted_iota(jnp.int32, (chunks, LANES), 0) * LANES
        + lax.broadcasted_iota(jnp.int32, (chunks, LANES), 1)
    )
    user_of = jnp.zeros((chunks, LANES), jnp.int32)
    for u in range(1, users):
        user_of = user_of + jnp.where(position >= u * slots, 1, 0)
    hi_iota = lax.broadcasted_iota(jnp.int32, (n_hi * users, LANES), 0)
    lo_iota = lax.broadcasted_iota(jnp.int32, (LANES, LANES), 0)
    used = users * slots // LANES

    def count_source(i):
        source = lax.rem(t + tables - i, tables)
        if isinstance(i, int):
            if i > 0:
                ids_copy(t, source, t).wait_recv()
        else:

            @pl.when(i > 0)
            def _():
                ids_copy(t, source, t).wait_recv()

        ids = got[source]
        hi_key = jnp.where(ids >= 0, (ids >> 7) * users + user_of, -1)
        lo_key = ids & (LANES - 1)
        hi_hot, lo_hot = [], []
        for c in range(used):
            hi_hot.append(jnp.where(hi_key[c : c + 1, :] == hi_iota, 1.0, 0.0).astype(BF16))
            lo_hot.append(jnp.where(lo_key[c : c + 1, :] == lo_iota, 1.0, 0.0).astype(BF16))
        block = dot_nt(jnp.concatenate(hi_hot, axis=1), jnp.concatenate(lo_hot, axis=1))
        block = block.astype(BF16)
        rows = pl.ds(pl.multiple_of(source * users, users), users)
        for h in range(n_hi):
            counts[rows, h * LANES : (h + 1) * LANES] = block[h * users : (h + 1) * users, :]

    each(tables, count_source)

    loads[0].wait()
    per_step = min(tables, 8)
    table_all = table_v[...]

    def pool_step(k):
        rows = per_step * users
        part = dot_nn(counts[pl.ds(k * rows, rows), :], table_all).astype(BF16)
        part_send[pl.ds(k * per_step, per_step)] = part.reshape(per_step, users, width)

    each(tables // per_step, pool_step)

    def part_copy(dst_table, owner, src_table):
        return pltpu.make_async_remote_copy(
            src_ref=part_send.at[src_table],
            dst_ref=part_recv.at[owner],
            send_sem=part_ssem.at[src_table],
            recv_sem=part_rsem.at[owner],
            device_id=(dst_table, s),
            device_id_type=MESH,
        )

    def send_part(i):
        peer = table_peer(i + 1)
        part_copy(peer, t, peer).start()

    each(tables - 1, send_part)
    part_recv[t] = part_send[t]

    loads[1].wait()
    loads[2].wait()
    loads[3].wait()
    items = item_v[...]
    half = width
    pre_item = dot_nn(items, wh_v[half:, :]) + bh_ref[...]
    cross_item = dot_nn(items, wc_v[half:, :]) + (bc_ref[...] + 1.0)

    def take_part(i):
        source = lax.rem(t + tables - 1 - i, tables)
        part_copy(t, source, t).wait_recv()

    each(tables - 1, take_part)
    pooled = jnp.sum(part_recv[...].astype(F32), axis=0) * scale
    pooled = pooled.astype(BF16)
    pool_all[s] = pooled

    def pool_copy(dst_sample, owner, sem):
        return pltpu.make_async_remote_copy(
            src_ref=pool_all.at[owner],
            dst_ref=pool_all.at[owner],
            send_sem=pool_ssem.at[sem],
            recv_sem=pool_rsem.at[owner],
            device_id=(t, dst_sample),
            device_id_type=MESH,
        )

    def send_pool(i):
        peer = sample_peer(i + 1)
        pool_copy(peer, s, peer).start()

    each(samples - 1, send_pool)
    pooled_out[...] = pooled

    def take_pool(i):
        source = lax.rem(s + samples - 1 - i, samples)
        pool_copy(s, source, s).wait_recv()

    each(samples - 1, take_pool)
    user_feat = dot_nn(picks, pool_all[...].reshape(group, width)).astype(BF16)

    pre = dot_nn(user_feat, wh_v[:half, :]) + pre_item
    cross = dot_nn(user_feat, wc_v[:half, :]) + cross_item
    pre_sq = pre * pre
    tanh = jnp.tanh(pre * (GELU_A + (GELU_A * GELU_B) * pre_sq))
    gate = 0.5 + 0.5 * tanh
    hidden = (pre * gate).astype(BF16)
    slope = gate + (0.5 * pre) * (1.0 - tanh * tanh) * (GELU_A + (3.0 * GELU_A * GELU_B) * pre_sq)
    loads[4].wait()
    lifted = jnp.concatenate([user_feat, items], axis=1).astype(F32)
    summed = dot_nn(hidden, wb_v[...]) + lifted * cross
    columns = 2 * width
    row_mean = jnp.sum(summed, axis=1, keepdims=True) * (1.0 / columns)
    centred = summed - row_mean
    row_var = jnp.sum(centred * centred, axis=1, keepdims=True) * (1.0 / columns)
    rstd = lax.rsqrt(row_var + 1e-05)
    raw_score = jnp.sum(centred * v_row, axis=1, keepdims=True)
    score = raw_score * rstd
    score_grad = jax.nn.sigmoid(score) - label_col
    pull = score_grad * rstd
    d_sum = pull * v_centred - centred * (pull * rstd * score * (1.0 / columns))
    d_hidden = dot_nt(d_sum.astype(BF16), wb_v[...]).astype(BF16).astype(F32)
    d_pre = (d_hidden * slope).astype(BF16)
    d_cross = (d_sum * lifted).astype(BF16)
    d_lift = d_sum * cross

    user_part = (
        d_lift[:, :half] + dot_nt(d_pre, wh_v[:half, :]) + dot_nt(d_cross, wc_v[:half, :])
    )
    per_user = dot_nn(picks_t, user_part.astype(BF16))
    grad_send[...] = per_user.astype(BF16).reshape(samples, users, width)

    def grad_copy(dst_sample, owner, src_sample):
        return pltpu.make_async_remote_copy(
            src_ref=grad_send.at[src_sample],
            dst_ref=grad_recv.at[owner],
            send_sem=grad_ssem.at[src_sample],
            recv_sem=grad_rsem.at[owner],
            device_id=(t, dst_sample),
            device_id_type=MESH,
        )

    def send_grad(i):
        peer = sample_peer(i + 1)
        grad_copy(peer, s, peer).start()

    each(samples - 1, send_grad)
    grad_recv[s] = grad_send[s]

    igrad_v[...] = (
        d_lift[:, half:] + dot_nt(d_pre, wh_v[half:, :]) + dot_nt(d_cross, wc_v[half:, :])
    )
    store = pltpu.make_async_copy(igrad_v, igrad_hbm, load_sem.at[5])
    store.start()
    scores_out[...] = jnp.transpose(jnp.broadcast_to(score, (imps, LANES)))[:1, :]

    def take_grad(i):
        source = lax.rem(s + samples - 1 - i, samples)
        grad_copy(s, source, s).wait_recv()

    each(samples - 1, take_grad)
    ugrad_out[...] = jnp.sum(grad_recv[...].astype(F32), axis=0)

    def sent_table(i):
        peer = table_peer(i + 1)
        ids_copy(peer, t, peer).wait_send()
        part_copy(peer, t, peer).wait_send()

    def sent_sample(i):
        peer = sample_peer(i + 1)
        pool_copy(peer, s, peer).wait_send()
        grad_copy(peer, s, peer).wait_send()

    each(tables - 1, sent_table)
    each(samples - 1, sent_sample)
    store.wait()


def body(tables, samples, *args):
    (
        hist_ids,
        hist_lens,
        table_rows,
        imp_user,
        item_rows,
        labels,
        w_hidden,
        b_hidden,
        w_back,
        w_cross,
        b_cross,
        norm_gain,
        w_score,
    ) = args
    users, _, slots = hist_ids.shape
    rows, width = table_rows.shape
    imps = item_rows.shape[0]
    history = slots * tables * 2 // 3
    assert (users * slots) % LANES == 0 and rows % LANES == 0 and users % 16 == 0
    chunks = -(-(users * slots // LANES) // 8) * 8
    vmem = pl.BlockSpec(memory_space=pltpu.VMEM)
    hbm = pl.BlockSpec(memory_space=pl.ANY)
    dma = pltpu.SemaphoreType.DMA

    def rowed(a):
        return a.reshape(1, -1)

    pooled, scores, user_grad, item_grad = pl.pallas_call(
        functools.partial(kernel, float(history) ** (-0.5)),
        out_shape=(
            jax.ShapeDtypeStruct((users, width), BF16),
            jax.ShapeDtypeStruct((1, imps), F32),
            jax.ShapeDtypeStruct((users, width), F32),
            jax.ShapeDtypeStruct((imps, width), F32),
        ),
        in_specs=[vmem, vmem, hbm, vmem, hbm, vmem, hbm, vmem, hbm, hbm, vmem, vmem, vmem],
        out_specs=(vmem, vmem, vmem, hbm),
        scratch_shapes=[
            pltpu.VMEM(table_rows.shape, BF16),
            pltpu.VMEM(item_rows.shape, BF16),
            pltpu.VMEM(w_hidden.shape, BF16),
            pltpu.VMEM(w_back.shape, BF16),
            pltpu.VMEM(w_cross.shape, BF16),
            pltpu.VMEM((tables, chunks, LANES), jnp.int32),
            pltpu.VMEM((tables, chunks, LANES), jnp.int32),
            pltpu.VMEM((tables * users, rows), BF16),
            pltpu.VMEM((tables, users, width), BF16),
            pltpu.VMEM((tables, users, width), BF16),
            pltpu.VMEM((samples, users, width), BF16),
            pltpu.VMEM((samples, users, width), BF16),
            pltpu.VMEM((samples, users, width), BF16),
            pltpu.VMEM((imps, width), F32),
            dma((6,)),
            dma((tables,)),
            dma((tables,)),
            dma((tables,)),
            dma((tables,)),
            dma((samples,)),
            dma((samples,)),
            dma((samples,)),
            dma((samples,)),
        ],
        compiler_params=pltpu.CompilerParams(
            collective_id=0, has_side_effects=True, vmem_limit_bytes=48 * 1024 * 1024
        ),
        cost_estimate=pl.CostEstimate(
            flops=1_500_000_000, bytes_accessed=4_000_000, transcendentals=200_000
        ),
    )(
        hist_ids,
        hist_lens,
        table_rows,
        rowed(imp_user),
        item_rows,
        rowed(labels),
        w_hidden,
        rowed(b_hidden),
        w_back,
        w_cross,
        rowed(b_cross),
        rowed(norm_gain),
        rowed(w_score),
    )
    return pooled, scores.reshape(imps), user_grad, item_grad


def solution(mesh):
    in_specs = (
        P(("table", "sample"), None, None),
        P(("table", "sample"), None),
        P("table", None),
        P(("table", "sample")),
        P(("table", "sample"), None),
        P(("table", "sample")),
        P(),
        P(),
        P(),
        P(),
        P(),
        P(),
        P(),
    )
    out_specs = (
        P(("table", "sample"), None),
        P(("table", "sample")),
        P(("table", "sample"), None),
        P(("table", "sample"), None),
    )
    step = functools.partial(body, mesh.shape["table"], mesh.shape["sample"])
    return jax.shard_map(step, mesh=mesh, in_specs=in_specs, out_specs=out_specs, check_vma=False)
```

```python
import functools

import jax
import jax.numpy as jnp
from jax import lax
from jax.experimental import pallas as pl
from jax.experimental.pallas import tpu as pltpu
from jax.sharding import PartitionSpec as P

MESH = pl.DeviceIdType.MESH
F32 = jnp.float32
BF16 = jnp.bfloat16
LANES = 128
VMEM_GRANT = 63 * 1024 * 1024
GELU_A = 0.7978845608028654
GELU_B = 0.044715


def dot_nn(a, b):
    return lax.dot_general(a, b, (((1,), (0,)), ((), ())), preferred_element_type=F32)


def dot_nt(a, b):
    return lax.dot_general(a, b, (((1,), (1,)), ((), ())), preferred_element_type=F32)


def to_column(row, width):
    return jnp.transpose(jnp.broadcast_to(row, (width, row.shape[1])))


def each(count, body):
    if count <= 8:
        for i in range(count):
            body(i)
    else:
        lax.fori_loop(0, count, lambda i, c: (body(i), c)[1], 0)


def kernel(
    scale,
    ids_hbm,
    lens_hbm,
    table_hbm,
    imp_hbm,
    item_hbm,
    label_hbm,
    wh_hbm,
    bh_hbm,
    wb_hbm,
    wc_hbm,
    bc_hbm,
    gain_hbm,
    ws_hbm,
    pooled_out,
    scores_out,
    ugrad_out,
    igrad_out,
    ids_ref,
    lens_ref,
    table_v,
    imp_ref,
    item_v,
    label_ref,
    wh_v,
    bh_ref,
    wb_v,
    wc_v,
    bc_ref,
    gain_ref,
    ws_ref,
    msg,
    got,
    counts,
    part_send,
    part_recv,
    pool_all,
    grad_send,
    grad_recv,
    igrad_v,
    scores_v,
    ugrad_v,
    load_sem,
    store_sem,
    ids_ssem,
    ids_rsem,
    part_ssem,
    part_rsem,
    pool_ssem,
    pool_rsem,
    grad_ssem,
    grad_rsem,
):
    tables, chunks = msg.shape[0], msg.shape[1]
    samples = pool_all.shape[0]
    users, _, slots = ids_ref.shape
    width = table_v.shape[1]
    n_hi = table_v.shape[0] // LANES
    imps = item_v.shape[0]
    group = samples * users
    t = lax.axis_index("table")
    s = lax.axis_index("sample")

    def table_peer(d):
        return lax.rem(t + d, tables)

    def sample_peer(d):
        return lax.rem(s + d, samples)

    barrier = pltpu.get_barrier_semaphore()

    def greet_table(i):
        pl.semaphore_signal(barrier, inc=1, device_id=(table_peer(i + 1), s), device_id_type=MESH)

    def greet_sample(i):
        pl.semaphore_signal(barrier, inc=1, device_id=(t, sample_peer(i + 1)), device_id_type=MESH)

    each(tables - 1, greet_table)
    each(samples - 1, greet_sample)

    pairs = dict(
        ids=(ids_hbm, ids_ref),
        lens=(lens_hbm, lens_ref),
        imp=(imp_hbm, imp_ref),
        label=(label_hbm, label_ref),
        gain=(gain_hbm, gain_ref),
        ws=(ws_hbm, ws_ref),
        table=(table_hbm, table_v),
        item=(item_hbm, item_v),
        bh=(bh_hbm, bh_ref),
        bc=(bc_hbm, bc_ref),
        wh=(wh_hbm, wh_v),
        wc=(wc_hbm, wc_v),
        wb=(wb_hbm, wb_v),
    )
    loads = {
        name: pltpu.make_async_copy(src, dst, load_sem.at[i])
        for i, (name, (src, dst)) in enumerate(pairs.items())
    }
    for load in loads.values():
        load.start()

    def arrived(*names):
        for name in names:
            loads[name].wait()

    arrived("ids", "lens")
    slot_iota = lax.broadcasted_iota(jnp.int32, (tables, slots), 1)
    pieces = []
    for u in range(users):
        pieces.append(jnp.where(slot_iota < lens_ref[:, u : u + 1], ids_ref[u], -1))
    packed = jnp.concatenate(pieces, axis=1)
    for c in range(users * slots // LANES):
        msg[:, c, :] = packed[:, c * LANES : (c + 1) * LANES]
    for c in range(users * slots // LANES, chunks):
        msg[:, c, :] = jnp.full((tables, LANES), -1, jnp.int32)

    pl.semaphore_wait(barrier, tables - 1 + samples - 1)

    def ids_copy(dst_table, owner, src_table):
        return pltpu.make_async_remote_copy(
            src_ref=msg.at[src_table],
            dst_ref=got.at[owner],
            send_sem=ids_ssem.at[src_table],
            recv_sem=ids_rsem.at[owner],
            device_id=(dst_table, s),
            device_id_type=MESH,
        )

    def send_ids(i):
        peer = table_peer(i + 1)
        ids_copy(peer, t, peer).start()

    each(tables - 1, send_ids)
    got[t] = msg[t]

    arrived("imp", "label", "gain", "ws")
    imp_row = imp_ref[...].astype(F32)
    imp_col = to_column(imp_row, LANES)[:, :1]
    picks = jnp.where(
        imp_col == lax.broadcasted_iota(jnp.int32, (imps, group), 1).astype(F32), 1.0, 0.0
    ).astype(BF16)
    picks_t = jnp.where(
        imp_ref[...] == lax.broadcasted_iota(jnp.int32, (group, imps), 0), 1.0, 0.0
    ).astype(BF16)
    label_col = to_column(label_ref[...].astype(F32), LANES)[:, :1]
    v_row = gain_ref[...] * ws_ref[...]
    v_centred = v_row - jnp.mean(v_row, axis=1, keepdims=True)

    position = (
        lax.broadcasted_iota(jnp.int32, (chunks, LANES), 0) * LANES
        + lax.broadcasted_iota(jnp.int32, (chunks, LANES), 1)
    )
    user_of = jnp.zeros((chunks, LANES), jnp.int32)
    for u in range(1, users):
        user_of = user_of + jnp.where(position >= u * slots, 1, 0)
    hi_iota = lax.broadcasted_iota(jnp.int32, (n_hi * users, LANES), 0).astype(F32).astype(BF16)
    lo_iota = hi_iota[:LANES]
    one, zero = jnp.ones((), BF16), jnp.zeros((), BF16)
    used = users * slots // LANES

    def count_source(i):
        source = lax.rem(t + tables - i, tables)
        if isinstance(i, int):
            if i > 0:
                ids_copy(t, source, t).wait_recv()
        else:

            @pl.when(i > 0)
            def _():
                ids_copy(t, source, t).wait_recv()

        ids = got[source]
        hi_key = jnp.where(ids >= 0, (ids >> 7) * users + user_of, -1).astype(F32).astype(BF16)
        lo_key = (ids & (LANES - 1)).astype(F32).astype(BF16)
        hi_hot, lo_hot = [], []
        for c in range(used):
            hi_hot.append(jnp.where(hi_key[c : c + 1, :] == hi_iota, one, zero))
            lo_hot.append(jnp.where(lo_key[c : c + 1, :] == lo_iota, one, zero))
        block = dot_nt(jnp.concatenate(hi_hot, axis=1), jnp.concatenate(lo_hot, axis=1))
        block = block.astype(BF16)
        rows = pl.ds(pl.multiple_of(source * users, users), users)
        for h in range(n_hi):
            counts[rows, h * LANES : (h + 1) * LANES] = block[h * users : (h + 1) * users, :]

    each(tables, count_source)

    arrived("table")
    per_step = min(tables, 8)
    table_all = table_v[...]

    def pool_step(k):
        rows = per_step * users
        part = dot_nn(counts[pl.ds(k * rows, rows), :], table_all).astype(BF16)
        part_send[pl.ds(k * per_step, per_step)] = part.reshape(per_step, users, width)

    each(tables // per_step, pool_step)

    def part_copy(dst_table, owner, src_table):
        return pltpu.make_async_remote_copy(
            src_ref=part_send.at[src_table],
            dst_ref=part_recv.at[owner],
            send_sem=part_ssem.at[src_table],
            recv_sem=part_rsem.at[owner],
            device_id=(dst_table, s),
            device_id_type=MESH,
        )

    def send_part(i):
        peer = table_peer(i + 1)
        part_copy(peer, t, peer).start()

    each(tables - 1, send_part)
    part_recv[t] = part_send[t]

    arrived("item", "wh", "wc", "bh", "bc")
    items = item_v[...]
    half = width
    pre_item = dot_nn(items, wh_v[half:, :]) + bh_ref[...]
    cross_item = dot_nn(items, wc_v[half:, :]) + (bc_ref[...] + 1.0)

    def take_part(i):
        source = lax.rem(t + tables - 1 - i, tables)
        part_copy(t, source, t).wait_recv()

    each(tables - 1, take_part)
    pooled = jnp.sum(part_recv[...].astype(F32), axis=0) * scale
    pooled = pooled.astype(BF16)
    pool_all[s] = pooled

    def pool_copy(dst_sample, owner, sem):
        return pltpu.make_async_remote_copy(
            src_ref=pool_all.at[owner],
            dst_ref=pool_all.at[owner],
            send_sem=pool_ssem.at[sem],
            recv_sem=pool_rsem.at[owner],
            device_id=(t, dst_sample),
            device_id_type=MESH,
        )

    def send_pool(i):
        peer = sample_peer(i + 1)
        pool_copy(peer, s, peer).start()

    each(samples - 1, send_pool)
    stores = [pltpu.make_async_copy(pool_all.at[s], pooled_out, store_sem.at[0])]
    stores[0].start()

    def take_pool(i):
        source = lax.rem(s + samples - 1 - i, samples)
        pool_copy(s, source, s).wait_recv()

    each(samples - 1, take_pool)
    user_feat = dot_nn(picks, pool_all[...].reshape(group, width)).astype(BF16)

    pre = dot_nn(user_feat, wh_v[:half, :]) + pre_item
    cross = dot_nn(user_feat, wc_v[:half, :]) + cross_item
    pre_sq = pre * pre
    tanh = jnp.tanh(pre * (GELU_A + (GELU_A * GELU_B) * pre_sq))
    gate = 0.5 + 0.5 * tanh
    hidden = (pre * gate).astype(BF16)
    slope = gate + (0.5 * pre) * (1.0 - tanh * tanh) * (GELU_A + (3.0 * GELU_A * GELU_B) * pre_sq)
    arrived("wb")
    lifted = jnp.concatenate([user_feat, items], axis=1).astype(F32)
    summed = dot_nn(hidden, wb_v[...]) + lifted * cross
    columns = 2 * width
    row_mean = jnp.sum(summed, axis=1, keepdims=True) * (1.0 / columns)
    centred = summed - row_mean
    row_var = jnp.sum(centred * centred, axis=1, keepdims=True) * (1.0 / columns)
    rstd = lax.rsqrt(row_var + 1e-05)
    raw_score = jnp.sum(centred * v_row, axis=1, keepdims=True)
    score = raw_score * rstd
    score_grad = jax.nn.sigmoid(score) - label_col
    pull = score_grad * rstd
    d_sum = pull * v_centred - centred * (pull * rstd * score * (1.0 / columns))
    d_hidden = dot_nt(d_sum.astype(BF16), wb_v[...]).astype(BF16).astype(F32)
    d_pre = (d_hidden * slope).astype(BF16)
    d_cross = (d_sum * lifted).astype(BF16)
    d_lift = d_sum * cross

    user_part = (
        d_lift[:, :half] + dot_nt(d_pre, wh_v[:half, :]) + dot_nt(d_cross, wc_v[:half, :])
    )
    per_user = dot_nn(picks_t, user_part.astype(BF16))
    grad_send[...] = per_user.astype(BF16).reshape(samples, users, width)

    def grad_copy(dst_sample, owner, src_sample):
        return pltpu.make_async_remote_copy(
            src_ref=grad_send.at[src_sample],
            dst_ref=grad_recv.at[owner],
            send_sem=grad_ssem.at[src_sample],
            recv_sem=grad_rsem.at[owner],
            device_id=(t, dst_sample),
            device_id_type=MESH,
        )

    def send_grad(i):
        peer = sample_peer(i + 1)
        grad_copy(peer, s, peer).start()

    each(samples - 1, send_grad)
    grad_recv[s] = grad_send[s]

    igrad_v[...] = (
        d_lift[:, half:] + dot_nt(d_pre, wh_v[half:, :]) + dot_nt(d_cross, wc_v[half:, :])
    )
    stores.append(pltpu.make_async_copy(igrad_v, igrad_out, store_sem.at[1]))
    stores[1].start()
    scores_v[...] = jnp.transpose(jnp.broadcast_to(score, (imps, LANES)))[:1, :]
    stores.append(pltpu.make_async_copy(scores_v, scores_out, store_sem.at[2]))
    stores[2].start()

    def take_grad(i):
        source = lax.rem(s + samples - 1 - i, samples)
        grad_copy(s, source, s).wait_recv()

    each(samples - 1, take_grad)
    ugrad_v[...] = jnp.sum(grad_recv[...].astype(F32), axis=0)
    stores.append(pltpu.make_async_copy(ugrad_v, ugrad_out, store_sem.at[3]))
    stores[3].start()

    def sent_table(i):
        peer = table_peer(i + 1)
        ids_copy(peer, t, peer).wait_send()
        part_copy(peer, t, peer).wait_send()

    def sent_sample(i):
        peer = sample_peer(i + 1)
        pool_copy(peer, s, peer).wait_send()
        grad_copy(peer, s, peer).wait_send()

    each(tables - 1, sent_table)
    each(samples - 1, sent_sample)
    for store in stores:
        store.wait()


def write_out(*refs):
    *arrays, sems = refs
    count = len(arrays) // 2
    jobs = []
    for src, dst in zip(arrays[:count], arrays[count:]):
        parts = 4 if src.shape[0] % 64 == 0 else 1
        rows = src.shape[0] // parts
        jobs += [(src.at[pl.ds(k * rows, rows)], dst.at[pl.ds(k * rows, rows)]) for k in range(parts)]
    copies = [pltpu.make_async_copy(*job, sems.at[i]) for i, job in enumerate(jobs)]
    for copy in copies:
        copy.start()
    for copy in copies:
        copy.wait()


def body(tables, samples, *args):
    (
        hist_ids,
        hist_lens,
        table_rows,
        imp_user,
        item_rows,
        labels,
        w_hidden,
        b_hidden,
        w_back,
        w_cross,
        b_cross,
        norm_gain,
        w_score,
    ) = args
    users, _, slots = hist_ids.shape
    rows, width = table_rows.shape
    imps = item_rows.shape[0]
    history = slots * tables * 2 // 3
    assert (users * slots) % LANES == 0 and rows % LANES == 0 and users % 16 == 0
    chunks = -(-(users * slots // LANES) // 8) * 8
    hbm = pl.BlockSpec(memory_space=pltpu.HBM)
    dma = pltpu.SemaphoreType.DMA

    def rowed(a):
        return a.reshape(1, -1)

    operands = (
        hist_ids,
        hist_lens.T,
        table_rows,
        rowed(imp_user),
        item_rows,
        rowed(labels),
        w_hidden,
        rowed(b_hidden),
        w_back,
        w_cross,
        rowed(b_cross),
        rowed(norm_gain),
        rowed(w_score),
    )
    shapes = (
        jax.ShapeDtypeStruct((users, width), BF16),
        jax.ShapeDtypeStruct((1, imps), F32),
        jax.ShapeDtypeStruct((users, width), F32),
        jax.ShapeDtypeStruct((imps, width), F32),
    )
    results = pl.pallas_call(
        functools.partial(kernel, float(history) ** (-0.5)),
        out_shape=shapes,
        in_specs=[hbm] * len(operands),
        out_specs=(hbm,) * len(shapes),
        scratch_shapes=[
            *[pltpu.VMEM(a.shape, a.dtype) for a in operands],
            pltpu.VMEM((tables, chunks, LANES), jnp.int32),
            pltpu.VMEM((tables, chunks, LANES), jnp.int32),
            pltpu.VMEM((tables * users, rows), BF16),
            pltpu.VMEM((tables, users, width), BF16),
            pltpu.VMEM((tables, users, width), BF16),
            pltpu.VMEM((samples, users, width), BF16),
            pltpu.VMEM((samples, users, width), BF16),
            pltpu.VMEM((samples, users, width), BF16),
            pltpu.VMEM((imps, width), F32),
            pltpu.VMEM((1, imps), F32),
            pltpu.VMEM((users, width), F32),
            dma((len(operands),)),
            dma((len(shapes),)),
            dma((tables,)),
            dma((tables,)),
            dma((tables,)),
            dma((tables,)),
            dma((samples,)),
            dma((samples,)),
            dma((samples,)),
            dma((samples,)),
        ],
        compiler_params=pltpu.CompilerParams(
            collective_id=0, has_side_effects=True, vmem_limit_bytes=VMEM_GRANT
        ),
        cost_estimate=pl.CostEstimate(
            flops=1_500_000_000, bytes_accessed=4_000_000, transcendentals=200_000
        ),
    )(*operands)
    pooled, scores, user_grad, item_grad = pl.pallas_call(
        write_out,
        out_shape=shapes,
        in_specs=[hbm] * len(shapes),
        out_specs=(hbm,) * len(shapes),
        scratch_shapes=[dma((4 * len(shapes),))],
        compiler_params=pltpu.CompilerParams(vmem_limit_bytes=VMEM_GRANT),
    )(*results)
    return pooled, scores.reshape(imps), user_grad, item_grad


def solution(mesh):
    in_specs = (
        P(("table", "sample"), None, None),
        P(("table", "sample"), None),
        P("table", None),
        P(("table", "sample")),
        P(("table", "sample"), None),
        P(("table", "sample")),
        P(),
        P(),
        P(),
        P(),
        P(),
        P(),
        P(),
    )
    out_specs = (
        P(("table", "sample"), None),
        P(("table", "sample")),
        P(("table", "sample"), None),
        P(("table", "sample"), None),
    )
    step = functools.partial(body, mesh.shape["table"], mesh.shape["sample"])
    return jax.shard_map(step, mesh=mesh, in_specs=in_specs, out_specs=out_specs, check_vma=False)
```

```python
import functools

import jax
import jax.numpy as jnp
from jax import lax
from jax.experimental import pallas as pl
from jax.experimental.pallas import tpu as pltpu
from jax.sharding import PartitionSpec as P

MESH = pl.DeviceIdType.MESH
F32 = jnp.float32
BF16 = jnp.bfloat16
LANES = 128
VMEM_GRANT = 63 * 1024 * 1024
GELU_A = 0.7978845608028654
GELU_B = 0.044715


def dot_nn(a, b):
    return lax.dot_general(a, b, (((1,), (0,)), ((), ())), preferred_element_type=F32)


def dot_nt(a, b):
    return lax.dot_general(a, b, (((1,), (1,)), ((), ())), preferred_element_type=F32)


def to_column(row, width):
    return jnp.transpose(jnp.broadcast_to(row, (width, row.shape[1])))


def by_rows(body, *arrays, rows=32):
    total = arrays[0].shape[0]
    step = rows if total % rows == 0 else total
    blocks = [body(*[a[k : k + step] for a in arrays]) for k in range(0, total, step)]
    return tuple(jnp.concatenate(parts, axis=0) for parts in zip(*blocks))


def each(count, body):
    if count <= 8:
        for i in range(count):
            body(i)
    else:
        lax.fori_loop(0, count, lambda i, c: (body(i), c)[1], 0)


def kernel(
    scale,
    ids_hbm,
    lens_hbm,
    table_hbm,
    imp_hbm,
    item_hbm,
    label_hbm,
    wh_hbm,
    bh_hbm,
    wb_hbm,
    wc_hbm,
    bc_hbm,
    gain_hbm,
    ws_hbm,
    pooled_out,
    scores_out,
    ugrad_out,
    igrad_out,
    ids_ref,
    lens_ref,
    table_v,
    imp_ref,
    item_v,
    label_ref,
    wh_v,
    bh_ref,
    wb_v,
    wc_v,
    bc_ref,
    gain_ref,
    ws_ref,
    msg,
    got,
    counts,
    part_send,
    part_recv,
    pool_all,
    grad_send,
    grad_recv,
    igrad_v,
    scores_v,
    ugrad_v,
    load_sem,
    store_sem,
    ids_ssem,
    ids_rsem,
    part_ssem,
    part_rsem,
    pool_ssem,
    pool_rsem,
    grad_ssem,
    grad_rsem,
):
    tables, chunks = msg.shape[0], msg.shape[1]
    samples = pool_all.shape[0]
    users, _, slots = ids_ref.shape
    width = table_v.shape[1]
    n_hi = table_v.shape[0] // LANES
    imps = item_v.shape[0]
    group = samples * users
    t = lax.axis_index("table")
    s = lax.axis_index("sample")

    def table_peer(d):
        return lax.rem(t + d, tables)

    def sample_peer(d):
        return lax.rem(s + d, samples)

    pairs = dict(
        ids=(ids_hbm, ids_ref),
        lens=(lens_hbm, lens_ref),
        imp=(imp_hbm, imp_ref),
        label=(label_hbm, label_ref),
        gain=(gain_hbm, gain_ref),
        ws=(ws_hbm, ws_ref),
        table=(table_hbm, table_v),
        item=(item_hbm, item_v),
        bh=(bh_hbm, bh_ref),
        bc=(bc_hbm, bc_ref),
        wh=(wh_hbm, wh_v),
        wc=(wc_hbm, wc_v),
        wb=(wb_hbm, wb_v),
    )
    loads = {
        name: pltpu.make_async_copy(src, dst, load_sem.at[i])
        for i, (name, (src, dst)) in enumerate(pairs.items())
    }
    loads["ids"].start()
    loads["lens"].start()

    barrier = pltpu.get_barrier_semaphore()

    def greet_table(i):
        pl.semaphore_signal(barrier, inc=1, device_id=(table_peer(i + 1), s), device_id_type=MESH)

    def greet_sample(i):
        pl.semaphore_signal(barrier, inc=1, device_id=(t, sample_peer(i + 1)), device_id_type=MESH)

    each(tables - 1, greet_table)
    each(samples - 1, greet_sample)

    for name, load in loads.items():
        if name not in ("ids", "lens"):
            load.start()

    def arrived(*names):
        for name in names:
            loads[name].wait()

    arrived("ids", "lens")
    slot_iota = lax.broadcasted_iota(jnp.int32, (tables, slots), 1)
    pieces = []
    for u in range(users):
        pieces.append(jnp.where(slot_iota < lens_ref[:, u : u + 1], ids_ref[u], -1))
    packed = jnp.concatenate(pieces, axis=1)
    for c in range(users * slots // LANES):
        msg[:, c, :] = packed[:, c * LANES : (c + 1) * LANES]
    for c in range(users * slots // LANES, chunks):
        msg[:, c, :] = jnp.full((tables, LANES), -1, jnp.int32)

    pl.semaphore_wait(barrier, tables - 1 + samples - 1)

    def ids_copy(dst_table, owner, src_table):
        return pltpu.make_async_remote_copy(
            src_ref=msg.at[src_table],
            dst_ref=got.at[owner],
            send_sem=ids_ssem.at[src_table],
            recv_sem=ids_rsem.at[owner],
            device_id=(dst_table, s),
            device_id_type=MESH,
        )

    def send_ids(i):
        peer = table_peer(i + 1)
        ids_copy(peer, t, peer).start()

    each(tables - 1, send_ids)
    got[t] = msg[t]

    arrived("imp", "label", "gain", "ws")
    imp_row = imp_ref[...].astype(F32)
    imp_col = to_column(imp_row, LANES)[:, :1]
    picks = jnp.where(
        imp_col == lax.broadcasted_iota(jnp.int32, (imps, group), 1).astype(F32), 1.0, 0.0
    ).astype(BF16)
    picks_t = jnp.where(
        imp_ref[...] == lax.broadcasted_iota(jnp.int32, (group, imps), 0), 1.0, 0.0
    ).astype(BF16)
    label_col = to_column(label_ref[...].astype(F32), LANES)[:, :1]
    v_row = gain_ref[...] * ws_ref[...]
    v_centred = v_row - jnp.mean(v_row, axis=1, keepdims=True)

    position = (
        lax.broadcasted_iota(jnp.int32, (chunks, LANES), 0) * LANES
        + lax.broadcasted_iota(jnp.int32, (chunks, LANES), 1)
    )
    user_of = jnp.zeros((chunks, LANES), jnp.int32)
    for u in range(1, users):
        user_of = user_of + jnp.where(position >= u * slots, 1, 0)
    hi_iota = lax.broadcasted_iota(jnp.int32, (n_hi * users, LANES), 0).astype(F32).astype(BF16)
    lo_iota = hi_iota[:LANES]
    one, zero = jnp.ones((), BF16), jnp.zeros((), BF16)
    used = users * slots // LANES

    def count_source(i):
        source = lax.rem(t + tables - i, tables)
        if isinstance(i, int):
            if i > 0:
                ids_copy(t, source, t).wait_recv()
        else:

            @pl.when(i > 0)
            def _():
                ids_copy(t, source, t).wait_recv()

        ids = got[source]
        hi_key = jnp.where(ids >= 0, (ids >> 7) * users + user_of, -1).astype(F32).astype(BF16)
        lo_key = (ids & (LANES - 1)).astype(F32).astype(BF16)
        hi_hot, lo_hot = [], []
        for c in range(used):
            hi_hot.append(jnp.where(hi_key[c : c + 1, :] == hi_iota, one, zero))
            lo_hot.append(jnp.where(lo_key[c : c + 1, :] == lo_iota, one, zero))
        block = dot_nt(jnp.concatenate(hi_hot, axis=1), jnp.concatenate(lo_hot, axis=1))
        block = block.astype(BF16)
        rows = pl.ds(pl.multiple_of(source * users, users), users)
        for h in range(n_hi):
            counts[rows, h * LANES : (h + 1) * LANES] = block[h * users : (h + 1) * users, :]

    each(tables, count_source)

    arrived("table")
    per_step = min(tables, 8)
    table_all = table_v[...]

    def pool_step(k):
        rows = per_step * users
        part = dot_nn(counts[pl.ds(k * rows, rows), :], table_all).astype(BF16)
        part_send[pl.ds(k * per_step, per_step)] = part.reshape(per_step, users, width)

    each(tables // per_step, pool_step)

    def part_copy(dst_table, owner, src_table):
        return pltpu.make_async_remote_copy(
            src_ref=part_send.at[src_table],
            dst_ref=part_recv.at[owner],
            send_sem=part_ssem.at[src_table],
            recv_sem=part_rsem.at[owner],
            device_id=(dst_table, s),
            device_id_type=MESH,
        )

    def send_part(i):
        peer = table_peer(i + 1)
        part_copy(peer, t, peer).start()

    each(tables - 1, send_part)
    part_recv[t] = part_send[t]

    arrived("item", "wh", "wc", "bh", "bc")
    items = item_v[...]
    half = width
    pre_item = dot_nn(items, wh_v[half:, :]) + bh_ref[...]
    cross_item = dot_nn(items, wc_v[half:, :]) + (bc_ref[...] + 1.0)

    def take_part(i):
        source = lax.rem(t + tables - 1 - i, tables)
        part_copy(t, source, t).wait_recv()

    each(tables - 1, take_part)
    pooled = jnp.sum(part_recv[...].astype(F32), axis=0) * scale
    pooled = pooled.astype(BF16)
    pool_all[s] = pooled

    def pool_copy(dst_sample, owner, sem):
        return pltpu.make_async_remote_copy(
            src_ref=pool_all.at[owner],
            dst_ref=pool_all.at[owner],
            send_sem=pool_ssem.at[sem],
            recv_sem=pool_rsem.at[owner],
            device_id=(t, dst_sample),
            device_id_type=MESH,
        )

    def send_pool(i):
        peer = sample_peer(i + 1)
        pool_copy(peer, s, peer).start()

    each(samples - 1, send_pool)
    stores = [pltpu.make_async_copy(pool_all.at[s], pooled_out, store_sem.at[0])]
    stores[0].start()

    def take_pool(i):
        source = lax.rem(s + samples - 1 - i, samples)
        pool_copy(s, source, s).wait_recv()

    each(samples - 1, take_pool)
    user_feat = dot_nn(picks, pool_all[...].reshape(group, width)).astype(BF16)

    pre_all = dot_nn(user_feat, wh_v[:half, :])
    cross_all = dot_nn(user_feat, wc_v[:half, :])
    columns = 2 * width
    lifted_all = jnp.concatenate([user_feat, items], axis=1)

    def activate(pre, pre_add):
        pre = pre + pre_add
        pre_sq = pre * pre
        tanh = jnp.tanh(pre * (GELU_A + (GELU_A * GELU_B) * pre_sq))
        gate = 0.5 + 0.5 * tanh
        rise = (0.5 * GELU_A) + (1.5 * GELU_A * GELU_B) * pre_sq
        slope = gate + pre * (1.0 - tanh * tanh) * rise
        return (pre * gate).astype(BF16), slope

    hidden, slope_all = by_rows(activate, pre_all, pre_item)
    arrived("wb")
    back = dot_nn(hidden, wb_v[...])

    def score_rows(back, cross, cross_add, lifted, label):
        lifted = lifted.astype(F32)
        cross = cross + cross_add
        summed = back + lifted * cross
        row_mean = jnp.sum(summed, axis=1, keepdims=True) * (1.0 / columns)
        centred = summed - row_mean
        row_var = jnp.sum(centred * centred, axis=1, keepdims=True) * (1.0 / columns)
        raw_score = jnp.sum(centred * v_row, axis=1, keepdims=True)
        rstd = lax.rsqrt(row_var + 1e-05)
        score = raw_score * rstd
        pull = (jax.nn.sigmoid(score) - label) * rstd
        d_sum = pull * v_centred - centred * (pull * rstd * score * (1.0 / columns))
        return score, d_sum.astype(BF16), (d_sum * lifted).astype(BF16), d_sum * cross

    score, d_sum, d_cross, d_lift = by_rows(
        score_rows, back, cross_all, cross_item, lifted_all, label_col
    )
    d_hidden = dot_nt(d_sum, wb_v[...])
    (d_pre,) = by_rows(
        lambda d, slope: ((d.astype(BF16).astype(F32) * slope).astype(BF16),), d_hidden, slope_all
    )

    user_part = (
        d_lift[:, :half] + dot_nt(d_pre, wh_v[:half, :]) + dot_nt(d_cross, wc_v[:half, :])
    )
    per_user = dot_nn(picks_t, user_part.astype(BF16))
    grad_send[...] = per_user.astype(BF16).reshape(samples, users, width)

    def grad_copy(dst_sample, owner, src_sample):
        return pltpu.make_async_remote_copy(
            src_ref=grad_send.at[src_sample],
            dst_ref=grad_recv.at[owner],
            send_sem=grad_ssem.at[src_sample],
            recv_sem=grad_rsem.at[owner],
            device_id=(t, dst_sample),
            device_id_type=MESH,
        )

    def send_grad(i):
        peer = sample_peer(i + 1)
        grad_copy(peer, s, peer).start()

    each(samples - 1, send_grad)
    grad_recv[s] = grad_send[s]

    igrad_v[...] = (
        d_lift[:, half:] + dot_nt(d_pre, wh_v[half:, :]) + dot_nt(d_cross, wc_v[half:, :])
    )
    stores.append(pltpu.make_async_copy(igrad_v, igrad_out, store_sem.at[1]))
    stores[1].start()
    scores_v[...] = jnp.transpose(jnp.broadcast_to(score, (imps, LANES)))[:1, :]
    stores.append(pltpu.make_async_copy(scores_v, scores_out, store_sem.at[2]))
    stores[2].start()

    def take_grad(i):
        source = lax.rem(s + samples - 1 - i, samples)
        grad_copy(s, source, s).wait_recv()

    each(samples - 1, take_grad)
    ugrad_v[...] = jnp.sum(grad_recv[...].astype(F32), axis=0)
    stores.append(pltpu.make_async_copy(ugrad_v, ugrad_out, store_sem.at[3]))
    stores[3].start()

    def sent_table(i):
        peer = table_peer(i + 1)
        ids_copy(peer, t, peer).wait_send()
        part_copy(peer, t, peer).wait_send()

    def sent_sample(i):
        peer = sample_peer(i + 1)
        pool_copy(peer, s, peer).wait_send()
        grad_copy(peer, s, peer).wait_send()

    each(tables - 1, sent_table)
    each(samples - 1, sent_sample)
    for store in stores:
        store.wait()


def write_out(*refs):
    *arrays, sems = refs
    count = len(arrays) // 3
    sources, targets, held = arrays[:count], arrays[count : 2 * count], arrays[2 * count :]
    loads = [pltpu.make_async_copy(sources[i], held[i], sems.at[0, i]) for i in range(count)]
    stores = [pltpu.make_async_copy(held[i], targets[i], sems.at[1, i]) for i in range(count)]
    for load in loads[::-1]:
        load.start()
    for load, store in zip(loads, stores):
        load.wait()
        store.start()
    for store in stores:
        store.wait()


def body(tables, samples, *args):
    (
        hist_ids,
        hist_lens,
        table_rows,
        imp_user,
        item_rows,
        labels,
        w_hidden,
        b_hidden,
        w_back,
        w_cross,
        b_cross,
        norm_gain,
        w_score,
    ) = args
    users, _, slots = hist_ids.shape
    rows, width = table_rows.shape
    imps = item_rows.shape[0]
    history = slots * tables * 2 // 3
    assert (users * slots) % LANES == 0 and rows % LANES == 0 and users % 16 == 0
    chunks = -(-(users * slots // LANES) // 8) * 8
    hbm = pl.BlockSpec(memory_space=pltpu.HBM)
    dma = pltpu.SemaphoreType.DMA

    def rowed(a):
        return a.reshape(1, -1)

    operands = (
        hist_ids,
        hist_lens.T,
        table_rows,
        rowed(imp_user),
        item_rows,
        rowed(labels),
        w_hidden,
        rowed(b_hidden),
        w_back,
        w_cross,
        rowed(b_cross),
        rowed(norm_gain),
        rowed(w_score),
    )
    shapes = (
        jax.ShapeDtypeStruct((users, width), BF16),
        jax.ShapeDtypeStruct((1, imps), F32),
        jax.ShapeDtypeStruct((users, width), F32),
        jax.ShapeDtypeStruct((imps, width), F32),
    )
    results = pl.pallas_call(
        functools.partial(kernel, float(history) ** (-0.5)),
        out_shape=shapes,
        in_specs=[hbm] * len(operands),
        out_specs=(hbm,) * len(shapes),
        scratch_shapes=[
            *[pltpu.VMEM(a.shape, a.dtype) for a in operands],
            pltpu.VMEM((tables, chunks, LANES), jnp.int32),
            pltpu.VMEM((tables, chunks, LANES), jnp.int32),
            pltpu.VMEM((tables * users, rows), BF16),
            pltpu.VMEM((tables, users, width), BF16),
            pltpu.VMEM((tables, users, width), BF16),
            pltpu.VMEM((samples, users, width), BF16),
            pltpu.VMEM((samples, users, width), BF16),
            pltpu.VMEM((samples, users, width), BF16),
            pltpu.VMEM((imps, width), F32),
            pltpu.VMEM((1, imps), F32),
            pltpu.VMEM((users, width), F32),
            dma((len(operands),)),
            dma((len(shapes),)),
            dma((tables,)),
            dma((tables,)),
            dma((tables,)),
            dma((tables,)),
            dma((samples,)),
            dma((samples,)),
            dma((samples,)),
            dma((samples,)),
        ],
        compiler_params=pltpu.CompilerParams(
            collective_id=0, has_side_effects=True, vmem_limit_bytes=VMEM_GRANT
        ),
        cost_estimate=pl.CostEstimate(
            flops=1_500_000_000, bytes_accessed=4_000_000, transcendentals=200_000
        ),
    )(*operands)
    pooled, scores, user_grad, item_grad = pl.pallas_call(
        write_out,
        out_shape=shapes,
        in_specs=[hbm] * len(shapes),
        out_specs=(hbm,) * len(shapes),
        scratch_shapes=[*[pltpu.VMEM(a.shape, a.dtype) for a in shapes], dma((2, len(shapes)))],
        compiler_params=pltpu.CompilerParams(vmem_limit_bytes=VMEM_GRANT),
    )(*results)
    return pooled, scores.reshape(imps), user_grad, item_grad


def solution(mesh):
    in_specs = (
        P(("table", "sample"), None, None),
        P(("table", "sample"), None),
        P("table", None),
        P(("table", "sample")),
        P(("table", "sample"), None),
        P(("table", "sample")),
        P(),
        P(),
        P(),
        P(),
        P(),
        P(),
        P(),
    )
    out_specs = (
        P(("table", "sample"), None),
        P(("table", "sample")),
        P(("table", "sample"), None),
        P(("table", "sample"), None),
    )
    step = functools.partial(body, mesh.shape["table"], mesh.shape["sample"])
    return jax.shard_map(step, mesh=mesh, in_specs=in_specs, out_specs=out_specs, check_vma=False)
```

```python
import functools

import jax
import jax.numpy as jnp
from jax import lax
from jax.experimental import pallas as pl
from jax.experimental.pallas import tpu as pltpu
from jax.sharding import PartitionSpec as P

MESH = pl.DeviceIdType.MESH
F32 = jnp.float32
BF16 = jnp.bfloat16
LANES = 128
VMEM_GRANT = 63 * 1024 * 1024
GELU_A = 0.7978845608028654
GELU_B = 0.044715


def dot_nn(a, b):
    return lax.dot_general(a, b, (((1,), (0,)), ((), ())), preferred_element_type=F32)


def dot_nt(a, b):
    return lax.dot_general(a, b, (((1,), (1,)), ((), ())), preferred_element_type=F32)


def to_column(row, width):
    return jnp.transpose(jnp.broadcast_to(row, (width, row.shape[1])))


def by_rows(body, *arrays, rows=32):
    total = arrays[0].shape[0]
    step = rows if total % rows == 0 else total
    blocks = [body(*[a[k : k + step] for a in arrays]) for k in range(0, total, step)]
    return tuple(jnp.concatenate(parts, axis=0) for parts in zip(*blocks))


def each(count, body):
    if count <= 8:
        for i in range(count):
            body(i)
    else:
        lax.fori_loop(0, count, lambda i, c: (body(i), c)[1], 0)


def kernel(
    scale,
    ids_hbm,
    lens_hbm,
    table_hbm,
    imp_hbm,
    item_hbm,
    label_hbm,
    wh_hbm,
    bh_hbm,
    wb_hbm,
    wc_hbm,
    bc_hbm,
    gain_hbm,
    ws_hbm,
    pooled_out,
    scores_out,
    ugrad_out,
    igrad_out,
    ids_ref,
    lens_ref,
    table_v,
    imp_ref,
    item_v,
    label_ref,
    wh_v,
    bh_ref,
    wb_v,
    wc_v,
    bc_ref,
    gain_ref,
    ws_ref,
    msg,
    got,
    counts,
    part_send,
    part_recv,
    pool_all,
    grad_send,
    grad_recv,
    igrad_v,
    scores_v,
    ugrad_v,
    wb_t,
    wh_t,
    wc_t,
    load_sem,
    store_sem,
    ids_ssem,
    ids_rsem,
    part_ssem,
    part_rsem,
    pool_ssem,
    pool_rsem,
    grad_ssem,
    grad_rsem,
):
    tables, chunks = msg.shape[0], msg.shape[1]
    samples = pool_all.shape[0]
    users, _, slots = ids_ref.shape
    width = table_v.shape[1]
    n_hi = table_v.shape[0] // LANES
    imps = item_v.shape[0]
    group = samples * users
    t = lax.axis_index("table")
    s = lax.axis_index("sample")

    def table_peer(d):
        return lax.rem(t + d, tables)

    def sample_peer(d):
        return lax.rem(s + d, samples)

    pairs = dict(
        ids=(ids_hbm, ids_ref),
        lens=(lens_hbm, lens_ref),
        imp=(imp_hbm, imp_ref),
        label=(label_hbm, label_ref),
        gain=(gain_hbm, gain_ref),
        ws=(ws_hbm, ws_ref),
        table=(table_hbm, table_v),
        item=(item_hbm, item_v),
        bh=(bh_hbm, bh_ref),
        bc=(bc_hbm, bc_ref),
        wh=(wh_hbm, wh_v),
        wc=(wc_hbm, wc_v),
        wb=(wb_hbm, wb_v),
    )
    loads = {
        name: pltpu.make_async_copy(src, dst, load_sem.at[i])
        for i, (name, (src, dst)) in enumerate(pairs.items())
    }
    loads["ids"].start()
    loads["lens"].start()

    barrier = pltpu.get_barrier_semaphore()

    def greet_table(i):
        pl.semaphore_signal(barrier, inc=1, device_id=(table_peer(i + 1), s), device_id_type=MESH)

    def greet_sample(i):
        pl.semaphore_signal(barrier, inc=1, device_id=(t, sample_peer(i + 1)), device_id_type=MESH)

    each(tables - 1, greet_table)
    each(samples - 1, greet_sample)

    for name, load in loads.items():
        if name not in ("ids", "lens"):
            load.start()

    def arrived(*names):
        for name in names:
            loads[name].wait()

    arrived("ids", "lens")
    slot_iota = lax.broadcasted_iota(jnp.int32, (tables, slots), 1)
    pieces = []
    for u in range(users):
        pieces.append(jnp.where(slot_iota < lens_ref[:, u : u + 1], ids_ref[u], -1))
    packed = jnp.concatenate(pieces, axis=1)
    for c in range(users * slots // LANES):
        msg[:, c, :] = packed[:, c * LANES : (c + 1) * LANES]
    for c in range(users * slots // LANES, chunks):
        msg[:, c, :] = jnp.full((tables, LANES), -1, jnp.int32)

    pl.semaphore_wait(barrier, tables - 1 + samples - 1)

    def ids_copy(dst_table, owner, src_table):
        return pltpu.make_async_remote_copy(
            src_ref=msg.at[src_table],
            dst_ref=got.at[owner],
            send_sem=ids_ssem.at[src_table],
            recv_sem=ids_rsem.at[owner],
            device_id=(dst_table, s),
            device_id_type=MESH,
        )

    def send_ids(i):
        peer = table_peer(i + 1)
        ids_copy(peer, t, peer).start()

    each(tables - 1, send_ids)
    got[t] = msg[t]

    arrived("imp", "label", "gain", "ws")
    imp_row = imp_ref[...].astype(F32)
    imp_col = to_column(imp_row, LANES)[:, :1]
    picks = jnp.where(
        imp_col == lax.broadcasted_iota(jnp.int32, (imps, group), 1).astype(F32), 1.0, 0.0
    ).astype(BF16)
    picks_t = jnp.where(
        imp_ref[...] == lax.broadcasted_iota(jnp.int32, (group, imps), 0), 1.0, 0.0
    ).astype(BF16)
    label_col = to_column(label_ref[...].astype(F32), LANES)[:, :1]
    v_row = gain_ref[...] * ws_ref[...]
    v_centred = v_row - jnp.mean(v_row, axis=1, keepdims=True)

    position = (
        lax.broadcasted_iota(jnp.int32, (chunks, LANES), 0) * LANES
        + lax.broadcasted_iota(jnp.int32, (chunks, LANES), 1)
    )
    user_of = jnp.zeros((chunks, LANES), jnp.int32)
    for u in range(1, users):
        user_of = user_of + jnp.where(position >= u * slots, 1, 0)
    hi_iota = lax.broadcasted_iota(jnp.int32, (n_hi * users, LANES), 0).astype(F32).astype(BF16)
    lo_iota = hi_iota[:LANES]
    one, zero = jnp.ones((), BF16), jnp.zeros((), BF16)
    used = users * slots // LANES

    def count_source(i):
        source = lax.rem(t + tables - i, tables)
        if isinstance(i, int):
            if i > 0:
                ids_copy(t, source, t).wait_recv()
        else:

            @pl.when(i > 0)
            def _():
                ids_copy(t, source, t).wait_recv()

        ids = got[source]
        hi_key = jnp.where(ids >= 0, (ids >> 7) * users + user_of, -1).astype(F32).astype(BF16)
        lo_key = (ids & (LANES - 1)).astype(F32).astype(BF16)
        hi_hot, lo_hot = [], []
        for c in range(used):
            hi_hot.append(jnp.where(hi_key[c : c + 1, :] == hi_iota, one, zero))
            lo_hot.append(jnp.where(lo_key[c : c + 1, :] == lo_iota, one, zero))
        block = dot_nt(jnp.concatenate(hi_hot, axis=1), jnp.concatenate(lo_hot, axis=1))
        block = block.astype(BF16)
        rows = pl.ds(pl.multiple_of(source * users, users), users)
        for h in range(n_hi):
            counts[rows, h * LANES : (h + 1) * LANES] = block[h * users : (h + 1) * users, :]

    each(tables, count_source)

    arrived("table")
    per_step = min(tables, 8)
    table_all = table_v[...]

    def pool_step(k):
        rows = per_step * users
        part = dot_nn(counts[pl.ds(k * rows, rows), :], table_all).astype(BF16)
        part_send[pl.ds(k * per_step, per_step)] = part.reshape(per_step, users, width)

    each(tables // per_step, pool_step)

    def part_copy(dst_table, owner, src_table):
        return pltpu.make_async_remote_copy(
            src_ref=part_send.at[src_table],
            dst_ref=part_recv.at[owner],
            send_sem=part_ssem.at[src_table],
            recv_sem=part_rsem.at[owner],
            device_id=(dst_table, s),
            device_id_type=MESH,
        )

    def send_part(i):
        peer = table_peer(i + 1)
        part_copy(peer, t, peer).start()

    each(tables - 1, send_part)
    part_recv[t] = part_send[t]

    arrived("item", "wh", "wc", "bh", "bc")
    items = item_v[...]
    half = width
    pre_item = dot_nn(items, wh_v[half:, :]) + bh_ref[...]
    cross_item = dot_nn(items, wc_v[half:, :]) + (bc_ref[...] + 1.0)

    def take_part(i):
        source = lax.rem(t + tables - 1 - i, tables)
        part_copy(t, source, t).wait_recv()

    each(tables - 1, take_part)
    pooled = jnp.sum(part_recv[...].astype(F32), axis=0) * scale
    pooled = pooled.astype(BF16)
    pool_all[s] = pooled

    def pool_copy(dst_sample, owner, sem):
        return pltpu.make_async_remote_copy(
            src_ref=pool_all.at[owner],
            dst_ref=pool_all.at[owner],
            send_sem=pool_ssem.at[sem],
            recv_sem=pool_rsem.at[owner],
            device_id=(t, dst_sample),
            device_id_type=MESH,
        )

    def send_pool(i):
        peer = sample_peer(i + 1)
        pool_copy(peer, s, peer).start()

    each(samples - 1, send_pool)
    stores = [pltpu.make_async_copy(pool_all.at[s], pooled_out, store_sem.at[0])]
    stores[0].start()
    arrived("wb")
    wb_t[...] = jnp.transpose(wb_v[...])
    wh_t[...] = jnp.transpose(wh_v[:half, :])
    wc_t[...] = jnp.transpose(wc_v[:half, :])

    def take_pool(i):
        source = lax.rem(s + samples - 1 - i, samples)
        pool_copy(s, source, s).wait_recv()

    each(samples - 1, take_pool)
    user_feat = dot_nn(picks, pool_all[...].reshape(group, width)).astype(BF16)

    pre_all = dot_nn(user_feat, wh_v[:half, :])
    cross_all = dot_nn(user_feat, wc_v[:half, :])
    columns = 2 * width
    lifted_all = jnp.concatenate([user_feat, items], axis=1)

    def activate(pre, pre_add):
        pre = pre + pre_add
        pre_sq = pre * pre
        tanh = jnp.tanh(pre * (GELU_A + (GELU_A * GELU_B) * pre_sq))
        gate = 0.5 + 0.5 * tanh
        rise = (0.5 * GELU_A) + (1.5 * GELU_A * GELU_B) * pre_sq
        slope = gate + pre * (1.0 - tanh * tanh) * rise
        return (pre * gate).astype(BF16), slope

    hidden, slope_all = by_rows(activate, pre_all, pre_item)
    back = dot_nn(hidden, wb_v[...])

    def score_rows(back, cross, cross_add, lifted, label):
        lifted = lifted.astype(F32)
        cross = cross + cross_add
        summed = back + lifted * cross
        row_mean = jnp.sum(summed, axis=1, keepdims=True) * (1.0 / columns)
        centred = summed - row_mean
        row_var = jnp.sum(centred * centred, axis=1, keepdims=True) * (1.0 / columns)
        raw_score = jnp.sum(centred * v_row, axis=1, keepdims=True)
        rstd = lax.rsqrt(row_var + 1e-05)
        score = raw_score * rstd
        pull = (jax.nn.sigmoid(score) - label) * rstd
        d_sum = pull * v_centred - centred * (pull * rstd * score * (1.0 / columns))
        return score, d_sum.astype(BF16), (d_sum * lifted).astype(BF16), d_sum * cross

    score, d_sum, d_cross, d_lift = by_rows(
        score_rows, back, cross_all, cross_item, lifted_all, label_col
    )
    d_hidden = dot_nn(d_sum, wb_t[...])
    (d_pre,) = by_rows(
        lambda d, slope: ((d.astype(BF16).astype(F32) * slope).astype(BF16),), d_hidden, slope_all
    )

    user_part = (
        d_lift[:, :half] + dot_nn(d_pre, wh_t[...]) + dot_nn(d_cross, wc_t[...])
    )
    per_user = dot_nn(picks_t, user_part.astype(BF16))
    grad_send[...] = per_user.astype(BF16).reshape(samples, users, width)

    def grad_copy(dst_sample, owner, src_sample):
        return pltpu.make_async_remote_copy(
            src_ref=grad_send.at[src_sample],
            dst_ref=grad_recv.at[owner],
            send_sem=grad_ssem.at[src_sample],
            recv_sem=grad_rsem.at[owner],
            device_id=(t, dst_sample),
            device_id_type=MESH,
        )

    def send_grad(i):
        peer = sample_peer(i + 1)
        grad_copy(peer, s, peer).start()

    each(samples - 1, send_grad)
    grad_recv[s] = grad_send[s]

    igrad_v[...] = (
        d_lift[:, half:] + dot_nt(d_pre, wh_v[half:, :]) + dot_nt(d_cross, wc_v[half:, :])
    )
    stores.append(pltpu.make_async_copy(igrad_v, igrad_out, store_sem.at[1]))
    stores[1].start()
    scores_v[...] = jnp.transpose(jnp.broadcast_to(score, (imps, LANES)))[:1, :]
    stores.append(pltpu.make_async_copy(scores_v, scores_out, store_sem.at[2]))
    stores[2].start()

    def take_grad(i):
        source = lax.rem(s + samples - 1 - i, samples)
        grad_copy(s, source, s).wait_recv()

    each(samples - 1, take_grad)
    ugrad_v[...] = jnp.sum(grad_recv[...].astype(F32), axis=0)
    stores.append(pltpu.make_async_copy(ugrad_v, ugrad_out, store_sem.at[3]))
    stores[3].start()

    def sent_table(i):
        peer = table_peer(i + 1)
        ids_copy(peer, t, peer).wait_send()
        part_copy(peer, t, peer).wait_send()

    def sent_sample(i):
        peer = sample_peer(i + 1)
        pool_copy(peer, s, peer).wait_send()
        grad_copy(peer, s, peer).wait_send()

    each(tables - 1, sent_table)
    each(samples - 1, sent_sample)
    for store in stores:
        store.wait()


def write_out(*refs):
    *arrays, sems = refs
    count = len(arrays) // 3
    sources, targets, held = arrays[:count], arrays[count : 2 * count], arrays[2 * count :]
    loads = [pltpu.make_async_copy(sources[i], held[i], sems.at[0, i]) for i in range(count)]
    stores = [pltpu.make_async_copy(held[i], targets[i], sems.at[1, i]) for i in range(count)]
    for load in loads[::-1]:
        load.start()
    for load, store in zip(loads, stores):
        load.wait()
        store.start()
    for store in stores:
        store.wait()


def body(tables, samples, *args):
    (
        hist_ids,
        hist_lens,
        table_rows,
        imp_user,
        item_rows,
        labels,
        w_hidden,
        b_hidden,
        w_back,
        w_cross,
        b_cross,
        norm_gain,
        w_score,
    ) = args
    users, _, slots = hist_ids.shape
    rows, width = table_rows.shape
    imps = item_rows.shape[0]
    history = slots * tables * 2 // 3
    assert (users * slots) % LANES == 0 and rows % LANES == 0 and users % 16 == 0
    chunks = -(-(users * slots // LANES) // 8) * 8
    hbm = pl.BlockSpec(memory_space=pltpu.HBM)
    dma = pltpu.SemaphoreType.DMA

    def rowed(a):
        return a.reshape(1, -1)

    operands = (
        hist_ids,
        hist_lens.T,
        table_rows,
        rowed(imp_user),
        item_rows,
        rowed(labels),
        w_hidden,
        rowed(b_hidden),
        w_back,
        w_cross,
        rowed(b_cross),
        rowed(norm_gain),
        rowed(w_score),
    )
    shapes = (
        jax.ShapeDtypeStruct((users, width), BF16),
        jax.ShapeDtypeStruct((1, imps), F32),
        jax.ShapeDtypeStruct((users, width), F32),
        jax.ShapeDtypeStruct((imps, width), F32),
    )
    results = pl.pallas_call(
        functools.partial(kernel, float(history) ** (-0.5)),
        out_shape=shapes,
        in_specs=[hbm] * len(operands),
        out_specs=(hbm,) * len(shapes),
        scratch_shapes=[
            *[pltpu.VMEM(a.shape, a.dtype) for a in operands],
            pltpu.VMEM((tables, chunks, LANES), jnp.int32),
            pltpu.VMEM((tables, chunks, LANES), jnp.int32),
            pltpu.VMEM((tables * users, rows), BF16),
            pltpu.VMEM((tables, users, width), BF16),
            pltpu.VMEM((tables, users, width), BF16),
            pltpu.VMEM((samples, users, width), BF16),
            pltpu.VMEM((samples, users, width), BF16),
            pltpu.VMEM((samples, users, width), BF16),
            pltpu.VMEM((imps, width), F32),
            pltpu.VMEM((1, imps), F32),
            pltpu.VMEM((users, width), F32),
            pltpu.VMEM(w_back.shape[::-1], BF16),
            pltpu.VMEM((w_hidden.shape[1], width), BF16),
            pltpu.VMEM((w_cross.shape[1], width), BF16),
            dma((len(operands),)),
            dma((len(shapes),)),
            dma((tables,)),
            dma((tables,)),
            dma((tables,)),
            dma((tables,)),
            dma((samples,)),
            dma((samples,)),
            dma((samples,)),
            dma((samples,)),
        ],
        compiler_params=pltpu.CompilerParams(
            collective_id=0, has_side_effects=True, vmem_limit_bytes=VMEM_GRANT
        ),
        cost_estimate=pl.CostEstimate(
            flops=1_500_000_000, bytes_accessed=4_000_000, transcendentals=200_000
        ),
    )(*operands)
    pooled, scores, user_grad, item_grad = pl.pallas_call(
        write_out,
        out_shape=shapes,
        in_specs=[hbm] * len(shapes),
        out_specs=(hbm,) * len(shapes),
        scratch_shapes=[*[pltpu.VMEM(a.shape, a.dtype) for a in shapes], dma((2, len(shapes)))],
        compiler_params=pltpu.CompilerParams(vmem_limit_bytes=VMEM_GRANT),
    )(*results)
    return pooled, scores.reshape(imps), user_grad, item_grad


def solution(mesh):
    in_specs = (
        P(("table", "sample"), None, None),
        P(("table", "sample"), None),
        P("table", None),
        P(("table", "sample")),
        P(("table", "sample"), None),
        P(("table", "sample")),
        P(),
        P(),
        P(),
        P(),
        P(),
        P(),
        P(),
    )
    out_specs = (
        P(("table", "sample"), None),
        P(("table", "sample")),
        P(("table", "sample"), None),
        P(("table", "sample"), None),
    )
    step = functools.partial(body, mesh.shape["table"], mesh.shape["sample"])
    return jax.shard_map(step, mesh=mesh, in_specs=in_specs, out_specs=out_specs, check_vma=False)
```

```python
import functools

import jax
import jax.numpy as jnp
from jax import lax
from jax.experimental import pallas as pl
from jax.experimental.pallas import tpu as pltpu
from jax.sharding import PartitionSpec as P

MESH = pl.DeviceIdType.MESH
F32 = jnp.float32
BF16 = jnp.bfloat16
LANES = 128
VMEM_GRANT = 63 * 1024 * 1024
GELU_A = 0.7978845608028654
GELU_B = 0.044715


def dot_nn(a, b):
    return lax.dot_general(a, b, (((1,), (0,)), ((), ())), preferred_element_type=F32)


def dot_nt(a, b):
    return lax.dot_general(a, b, (((1,), (1,)), ((), ())), preferred_element_type=F32)


def to_column(row, width):
    return jnp.transpose(jnp.broadcast_to(row, (width, row.shape[1])))


def by_rows(body, *arrays, rows=32):
    total = arrays[0].shape[0]
    step = rows if total % rows == 0 else total
    blocks = [body(*[a[k : k + step] for a in arrays]) for k in range(0, total, step)]
    return tuple(jnp.concatenate(parts, axis=0) for parts in zip(*blocks))


def each(count, body):
    if count <= 8:
        for i in range(count):
            body(i)
    else:
        lax.fori_loop(0, count, lambda i, c: (body(i), c)[1], 0)


def kernel(
    scale,
    ids_hbm,
    lens_hbm,
    table_hbm,
    imp_hbm,
    item_hbm,
    label_hbm,
    wh_hbm,
    bh_hbm,
    wb_hbm,
    wc_hbm,
    bc_hbm,
    gain_hbm,
    ws_hbm,
    pooled_out,
    scores_out,
    ugrad_out,
    igrad_out,
    ids_ref,
    lens_ref,
    table_v,
    imp_ref,
    item_v,
    label_ref,
    wh_v,
    bh_ref,
    wb_v,
    wc_v,
    bc_ref,
    gain_ref,
    ws_ref,
    msg,
    got,
    counts,
    part_send,
    part_recv,
    pool_all,
    grad_send,
    grad_recv,
    igrad_v,
    scores_v,
    ugrad_v,
    wb_t,
    wh_t,
    wc_t,
    load_sem,
    store_sem,
    ids_ssem,
    ids_rsem,
    part_ssem,
    part_rsem,
    pool_ssem,
    pool_rsem,
    grad_ssem,
    grad_rsem,
):
    tables, chunks = msg.shape[0], msg.shape[1]
    samples = pool_all.shape[0]
    users, _, slots = ids_ref.shape
    width = table_v.shape[1]
    n_hi = table_v.shape[0] // LANES
    imps = item_v.shape[0]
    group = samples * users
    t = lax.axis_index("table")
    s = lax.axis_index("sample")

    def table_peer(d):
        return lax.rem(t + d, tables)

    def sample_peer(d):
        return lax.rem(s + d, samples)

    pairs = dict(
        ids=(ids_hbm, ids_ref),
        lens=(lens_hbm, lens_ref),
        imp=(imp_hbm, imp_ref),
        label=(label_hbm, label_ref),
        gain=(gain_hbm, gain_ref),
        ws=(ws_hbm, ws_ref),
        table=(table_hbm, table_v),
        item=(item_hbm, item_v),
        bh=(bh_hbm, bh_ref),
        bc=(bc_hbm, bc_ref),
        wh=(wh_hbm, wh_v),
        wc=(wc_hbm, wc_v),
        wb=(wb_hbm, wb_v),
    )
    loads = {
        name: pltpu.make_async_copy(src, dst, load_sem.at[i])
        for i, (name, (src, dst)) in enumerate(pairs.items())
    }
    loads["ids"].start()
    loads["lens"].start()

    barrier = pltpu.get_barrier_semaphore()

    def greet_table(i):
        pl.semaphore_signal(barrier, inc=1, device_id=(table_peer(i + 1), s), device_id_type=MESH)

    def greet_sample(i):
        pl.semaphore_signal(barrier, inc=1, device_id=(t, sample_peer(i + 1)), device_id_type=MESH)

    each(tables - 1, greet_table)
    each(samples - 1, greet_sample)

    for name, load in loads.items():
        if name not in ("ids", "lens"):
            load.start()

    def arrived(*names):
        for name in names:
            loads[name].wait()

    arrived("ids", "lens")
    slot_iota = lax.broadcasted_iota(jnp.int32, (tables, slots), 1)
    pieces = []
    for u in range(users):
        pieces.append(jnp.where(slot_iota < lens_ref[:, u : u + 1], ids_ref[u], -1))
    packed = jnp.concatenate(pieces, axis=1)
    for c in range(users * slots // LANES):
        msg[:, c, :] = packed[:, c * LANES : (c + 1) * LANES]
    for c in range(users * slots // LANES, chunks):
        msg[:, c, :] = jnp.full((tables, LANES), -1, jnp.int32)

    pl.semaphore_wait(barrier, tables - 1 + samples - 1)

    def ids_copy(dst_table, owner, src_table):
        return pltpu.make_async_remote_copy(
            src_ref=msg.at[src_table],
            dst_ref=got.at[owner],
            send_sem=ids_ssem.at[src_table],
            recv_sem=ids_rsem.at[owner],
            device_id=(dst_table, s),
            device_id_type=MESH,
        )

    def send_ids(i):
        peer = table_peer(i + 1)
        ids_copy(peer, t, peer).start()

    each(tables - 1, send_ids)
    got[t] = msg[t]

    arrived("imp", "label", "gain", "ws")
    imp_row = imp_ref[...].astype(F32)
    imp_col = to_column(imp_row, LANES)[:, :1]
    picks = jnp.where(
        imp_col == lax.broadcasted_iota(jnp.int32, (imps, group), 1).astype(F32), 1.0, 0.0
    ).astype(BF16)
    picks_t = jnp.where(
        imp_ref[...] == lax.broadcasted_iota(jnp.int32, (group, imps), 0), 1.0, 0.0
    ).astype(BF16)
    label_col = to_column(label_ref[...].astype(F32), LANES)[:, :1]
    v_row = gain_ref[...] * ws_ref[...]
    v_centred = v_row - jnp.mean(v_row, axis=1, keepdims=True)

    position = (
        lax.broadcasted_iota(jnp.int32, (chunks, LANES), 0) * LANES
        + lax.broadcasted_iota(jnp.int32, (chunks, LANES), 1)
    )
    user_of = jnp.zeros((chunks, LANES), jnp.int32)
    for u in range(1, users):
        user_of = user_of + jnp.where(position >= u * slots, 1, 0)
    user_of = jnp.where(user_of >= users // 2, user_of - users // 2, user_of)
    hi_iota = lax.broadcasted_iota(jnp.int32, (n_hi * users // 2, LANES), 0).astype(F32).astype(BF16)
    lo_iota = hi_iota[:LANES]
    one, zero = jnp.ones((), BF16), jnp.zeros((), BF16)
    used = users * slots // LANES

    def count_source(i):
        source = lax.rem(t + tables - i, tables)
        if isinstance(i, int):
            if i > 0:
                ids_copy(t, source, t).wait_recv()
        else:

            @pl.when(i > 0)
            def _():
                ids_copy(t, source, t).wait_recv()

        ids = got[source]
        hi_key = jnp.where(ids >= 0, (ids >> 7) * (users // 2) + user_of, -1).astype(F32).astype(BF16)
        lo_key = (ids & (LANES - 1)).astype(F32).astype(BF16)
        hi_hot, lo_hot = [], []
        for c in range(used):
            hi_hot.append(jnp.where(hi_key[c : c + 1, :] == hi_iota, one, zero))
            lo_hot.append(jnp.where(lo_key[c : c + 1, :] == lo_iota, one, zero))
        few, cut = users // 2, used // 2
        top, bottom = [
            dot_nt(
                jnp.concatenate(hi_hot[k : k + cut], axis=1),
                jnp.concatenate(lo_hot[k : k + cut], axis=1),
            )
            for k in (0, cut)
        ]
        rows = pl.ds(pl.multiple_of(source * users, users), users)
        for h in range(n_hi):
            own = slice(h * few, (h + 1) * few)
            both = jnp.concatenate([top[own], bottom[own]], axis=0)
            counts[rows, h * LANES : (h + 1) * LANES] = both.astype(BF16)

    each(tables, count_source)

    arrived("table")
    per_step = min(tables, 8)
    table_all = table_v[...]

    def pool_step(k):
        rows = per_step * users
        part = dot_nn(counts[pl.ds(k * rows, rows), :], table_all).astype(BF16)
        part_send[pl.ds(k * per_step, per_step)] = part.reshape(per_step, users, width)

    each(tables // per_step, pool_step)

    def part_copy(dst_table, owner, src_table):
        return pltpu.make_async_remote_copy(
            src_ref=part_send.at[src_table],
            dst_ref=part_recv.at[owner],
            send_sem=part_ssem.at[src_table],
            recv_sem=part_rsem.at[owner],
            device_id=(dst_table, s),
            device_id_type=MESH,
        )

    def send_part(i):
        peer = table_peer(i + 1)
        part_copy(peer, t, peer).start()

    each(tables - 1, send_part)
    part_recv[t] = part_send[t]

    arrived("item", "wh", "wc", "bh", "bc")
    items = item_v[...]
    half = width
    pre_item = dot_nn(items, wh_v[half:, :]) + bh_ref[...]
    cross_item = dot_nn(items, wc_v[half:, :]) + (bc_ref[...] + 1.0)

    def take_part(i):
        source = lax.rem(t + tables - 1 - i, tables)
        part_copy(t, source, t).wait_recv()

    each(tables - 1, take_part)
    pooled = jnp.sum(part_recv[...].astype(F32), axis=0) * scale
    pooled = pooled.astype(BF16)
    pool_all[s] = pooled

    def pool_copy(dst_sample, owner, sem):
        return pltpu.make_async_remote_copy(
            src_ref=pool_all.at[owner],
            dst_ref=pool_all.at[owner],
            send_sem=pool_ssem.at[sem],
            recv_sem=pool_rsem.at[owner],
            device_id=(t, dst_sample),
            device_id_type=MESH,
        )

    def send_pool(i):
        peer = sample_peer(i + 1)
        pool_copy(peer, s, peer).start()

    each(samples - 1, send_pool)
    stores = [pltpu.make_async_copy(pool_all.at[s], pooled_out, store_sem.at[0])]
    stores[0].start()
    arrived("wb")
    wb_t[...] = jnp.transpose(wb_v[...])
    wh_t[...] = jnp.transpose(wh_v[:half, :])
    wc_t[...] = jnp.transpose(wc_v[:half, :])

    def take_pool(i):
        source = lax.rem(s + samples - 1 - i, samples)
        pool_copy(s, source, s).wait_recv()

    each(samples - 1, take_pool)
    user_feat = dot_nn(picks, pool_all[...].reshape(group, width)).astype(BF16)

    pre_all = dot_nn(user_feat, wh_v[:half, :])
    cross_all = dot_nn(user_feat, wc_v[:half, :])
    columns = 2 * width
    lifted_all = jnp.concatenate([user_feat, items], axis=1)

    def activate(pre, pre_add):
        pre = pre + pre_add
        pre_sq = pre * pre
        tanh = jnp.tanh(pre * (GELU_A + (GELU_A * GELU_B) * pre_sq))
        gate = 0.5 + 0.5 * tanh
        rise = (0.5 * GELU_A) + (1.5 * GELU_A * GELU_B) * pre_sq
        slope = gate + pre * (1.0 - tanh * tanh) * rise
        return (pre * gate).astype(BF16), slope

    hidden, slope_all = by_rows(activate, pre_all, pre_item)
    back = dot_nn(hidden, wb_v[...])

    def score_rows(back, cross, cross_add, lifted, label):
        lifted = lifted.astype(F32)
        cross = cross + cross_add
        summed = back + lifted * cross
        row_mean = jnp.sum(summed, axis=1, keepdims=True) * (1.0 / columns)
        centred = summed - row_mean
        row_var = jnp.sum(centred * centred, axis=1, keepdims=True) * (1.0 / columns)
        raw_score = jnp.sum(centred * v_row, axis=1, keepdims=True)
        rstd = lax.rsqrt(row_var + 1e-05)
        score = raw_score * rstd
        pull = (jax.nn.sigmoid(score) - label) * rstd
        d_sum = pull * v_centred - centred * (pull * rstd * score * (1.0 / columns))
        return score, d_sum.astype(BF16), (d_sum * lifted).astype(BF16), d_sum * cross

    score, d_sum, d_cross, d_lift = by_rows(
        score_rows, back, cross_all, cross_item, lifted_all, label_col
    )
    d_hidden = dot_nn(d_sum, wb_t[...])
    (d_pre,) = by_rows(
        lambda d, slope: ((d.astype(BF16).astype(F32) * slope).astype(BF16),), d_hidden, slope_all
    )

    user_part = (
        d_lift[:, :half] + dot_nn(d_pre, wh_t[...]) + dot_nn(d_cross, wc_t[...])
    )
    per_user = dot_nn(picks_t, user_part.astype(BF16))
    grad_send[...] = per_user.astype(BF16).reshape(samples, users, width)

    def grad_copy(dst_sample, owner, src_sample):
        return pltpu.make_async_remote_copy(
            src_ref=grad_send.at[src_sample],
            dst_ref=grad_recv.at[owner],
            send_sem=grad_ssem.at[src_sample],
            recv_sem=grad_rsem.at[owner],
            device_id=(t, dst_sample),
            device_id_type=MESH,
        )

    def send_grad(i):
        peer = sample_peer(i + 1)
        grad_copy(peer, s, peer).start()

    each(samples - 1, send_grad)
    grad_recv[s] = grad_send[s]

    igrad_v[...] = (
        d_lift[:, half:] + dot_nt(d_pre, wh_v[half:, :]) + dot_nt(d_cross, wc_v[half:, :])
    )
    stores.append(pltpu.make_async_copy(igrad_v, igrad_out, store_sem.at[1]))
    stores[1].start()
    scores_v[...] = jnp.transpose(jnp.broadcast_to(score, (imps, LANES)))[:1, :]
    stores.append(pltpu.make_async_copy(scores_v, scores_out, store_sem.at[2]))
    stores[2].start()

    def take_grad(i):
        source = lax.rem(s + samples - 1 - i, samples)
        grad_copy(s, source, s).wait_recv()

    each(samples - 1, take_grad)
    ugrad_v[...] = jnp.sum(grad_recv[...].astype(F32), axis=0)
    stores.append(pltpu.make_async_copy(ugrad_v, ugrad_out, store_sem.at[3]))
    stores[3].start()

    def sent_table(i):
        peer = table_peer(i + 1)
        ids_copy(peer, t, peer).wait_send()
        part_copy(peer, t, peer).wait_send()

    def sent_sample(i):
        peer = sample_peer(i + 1)
        pool_copy(peer, s, peer).wait_send()
        grad_copy(peer, s, peer).wait_send()

    each(tables - 1, sent_table)
    each(samples - 1, sent_sample)
    for store in stores:
        store.wait()


def write_out(*refs):
    *arrays, sems = refs
    count = len(arrays) // 3
    sources, targets, held = arrays[:count], arrays[count : 2 * count], arrays[2 * count :]
    loads = [pltpu.make_async_copy(sources[i], held[i], sems.at[0, i]) for i in range(count)]
    stores = [pltpu.make_async_copy(held[i], targets[i], sems.at[1, i]) for i in range(count)]
    for load in loads[::-1]:
        load.start()
    for load, store in zip(loads, stores):
        load.wait()
        store.start()
    for store in stores:
        store.wait()


def body(tables, samples, *args):
    (
        hist_ids,
        hist_lens,
        table_rows,
        imp_user,
        item_rows,
        labels,
        w_hidden,
        b_hidden,
        w_back,
        w_cross,
        b_cross,
        norm_gain,
        w_score,
    ) = args
    users, _, slots = hist_ids.shape
    rows, width = table_rows.shape
    imps = item_rows.shape[0]
    history = slots * tables * 2 // 3
    assert (users * slots) % (2 * LANES) == 0 and rows % LANES == 0 and users % 16 == 0
    chunks = -(-(users * slots // LANES) // 8) * 8
    hbm = pl.BlockSpec(memory_space=pltpu.HBM)
    dma = pltpu.SemaphoreType.DMA

    def rowed(a):
        return a.reshape(1, -1)

    operands = (
        hist_ids,
        hist_lens.T,
        table_rows,
        rowed(imp_user),
        item_rows,
        rowed(labels),
        w_hidden,
        rowed(b_hidden),
        w_back,
        w_cross,
        rowed(b_cross),
        rowed(norm_gain),
        rowed(w_score),
    )
    shapes = (
        jax.ShapeDtypeStruct((users, width), BF16),
        jax.ShapeDtypeStruct((1, imps), F32),
        jax.ShapeDtypeStruct((users, width), F32),
        jax.ShapeDtypeStruct((imps, width), F32),
    )
    results = pl.pallas_call(
        functools.partial(kernel, float(history) ** (-0.5)),
        out_shape=shapes,
        in_specs=[hbm] * len(operands),
        out_specs=(hbm,) * len(shapes),
        scratch_shapes=[
            *[pltpu.VMEM(a.shape, a.dtype) for a in operands],
            pltpu.VMEM((tables, chunks, LANES), jnp.int32),
            pltpu.VMEM((tables, chunks, LANES), jnp.int32),
            pltpu.VMEM((tables * users, rows), BF16),
            pltpu.VMEM((tables, users, width), BF16),
            pltpu.VMEM((tables, users, width), BF16),
            pltpu.VMEM((samples, users, width), BF16),
            pltpu.VMEM((samples, users, width), BF16),
            pltpu.VMEM((samples, users, width), BF16),
            pltpu.VMEM((imps, width), F32),
            pltpu.VMEM((1, imps), F32),
            pltpu.VMEM((users, width), F32),
            pltpu.VMEM(w_back.shape[::-1], BF16),
            pltpu.VMEM((w_hidden.shape[1], width), BF16),
            pltpu.VMEM((w_cross.shape[1], width), BF16),
            dma((len(operands),)),
            dma((len(shapes),)),
            dma((tables,)),
            dma((tables,)),
            dma((tables,)),
            dma((tables,)),
            dma((samples,)),
            dma((samples,)),
            dma((samples,)),
            dma((samples,)),
        ],
        compiler_params=pltpu.CompilerParams(
            collective_id=0, has_side_effects=True, vmem_limit_bytes=VMEM_GRANT
        ),
        cost_estimate=pl.CostEstimate(
            flops=1_500_000_000, bytes_accessed=4_000_000, transcendentals=200_000
        ),
    )(*operands)
    pooled, scores, user_grad, item_grad = pl.pallas_call(
        write_out,
        out_shape=shapes,
        in_specs=[hbm] * len(shapes),
        out_specs=(hbm,) * len(shapes),
        scratch_shapes=[*[pltpu.VMEM(a.shape, a.dtype) for a in shapes], dma((2, len(shapes)))],
        compiler_params=pltpu.CompilerParams(vmem_limit_bytes=VMEM_GRANT),
    )(*results)
    return pooled, scores.reshape(imps), user_grad, item_grad


def solution(mesh):
    in_specs = (
        P(("table", "sample"), None, None),
        P(("table", "sample"), None),
        P("table", None),
        P(("table", "sample")),
        P(("table", "sample"), None),
        P(("table", "sample")),
        P(),
        P(),
        P(),
        P(),
        P(),
        P(),
        P(),
    )
    out_specs = (
        P(("table", "sample"), None),
        P(("table", "sample")),
        P(("table", "sample"), None),
        P(("table", "sample"), None),
    )
    step = functools.partial(body, mesh.shape["table"], mesh.shape["sample"])
    return jax.shard_map(step, mesh=mesh, in_specs=in_specs, out_specs=out_specs, check_vma=False)
```

```python
import functools

import jax
import jax.numpy as jnp
from jax import lax
from jax.experimental import pallas as pl
from jax.experimental.pallas import tpu as pltpu
from jax.sharding import PartitionSpec as P

MESH = pl.DeviceIdType.MESH
F32 = jnp.float32
BF16 = jnp.bfloat16
LANES = 128
VMEM_GRANT = 63 * 1024 * 1024
GELU_A = 0.7978845608028654
GELU_B = 0.044715


def dot_nn(a, b):
    return lax.dot_general(a, b, (((1,), (0,)), ((), ())), preferred_element_type=F32)


def dot_nt(a, b):
    return lax.dot_general(a, b, (((1,), (1,)), ((), ())), preferred_element_type=F32)


def to_column(row, width):
    return jnp.transpose(jnp.broadcast_to(row, (width, row.shape[1])))


def by_rows(body, *arrays, rows=32):
    total = arrays[0].shape[0]
    step = rows if total % rows == 0 else total
    blocks = [body(*[a[k : k + step] for a in arrays]) for k in range(0, total, step)]
    return tuple(jnp.concatenate(parts, axis=0) for parts in zip(*blocks))


def each(count, body):
    if count <= 8:
        for i in range(count):
            body(i)
    else:
        lax.fori_loop(0, count, lambda i, c: (body(i), c)[1], 0)


def kernel(
    scale,
    ids_hbm,
    lens_hbm,
    table_hbm,
    imp_hbm,
    item_hbm,
    label_hbm,
    wh_hbm,
    bh_hbm,
    wb_hbm,
    wc_hbm,
    bc_hbm,
    gain_hbm,
    ws_hbm,
    pooled_out,
    scores_out,
    ugrad_out,
    igrad_out,
    ids_ref,
    lens_ref,
    table_v,
    imp_ref,
    item_v,
    label_ref,
    wh_v,
    bh_ref,
    wb_v,
    wc_v,
    bc_ref,
    gain_ref,
    ws_ref,
    msg,
    got,
    counts,
    part_send,
    part_recv,
    pool_all,
    grad_send,
    grad_recv,
    igrad_v,
    scores_v,
    ugrad_v,
    wb_t,
    wh_t,
    wc_t,
    load_sem,
    store_sem,
    ids_ssem,
    ids_rsem,
    part_ssem,
    part_rsem,
    pool_ssem,
    pool_rsem,
    grad_ssem,
    grad_rsem,
):
    tables, chunks = msg.shape[0], msg.shape[1]
    samples = pool_all.shape[0]
    users, _, slots = ids_ref.shape
    width = table_v.shape[1]
    n_hi = table_v.shape[0] // LANES
    imps = item_v.shape[0]
    group = samples * users
    t = lax.axis_index("table")
    s = lax.axis_index("sample")

    def table_peer(d):
        return lax.rem(t + d, tables)

    def sample_peer(d):
        return lax.rem(s + d, samples)

    pairs = dict(
        ids=(ids_hbm, ids_ref),
        lens=(lens_hbm, lens_ref),
        imp=(imp_hbm, imp_ref),
        label=(label_hbm, label_ref),
        gain=(gain_hbm, gain_ref),
        ws=(ws_hbm, ws_ref),
        table=(table_hbm, table_v),
        item=(item_hbm, item_v),
        bh=(bh_hbm, bh_ref),
        bc=(bc_hbm, bc_ref),
        wh=(wh_hbm, wh_v),
        wc=(wc_hbm, wc_v),
        wb=(wb_hbm, wb_v),
    )
    loads = {
        name: pltpu.make_async_copy(src, dst, load_sem.at[i])
        for i, (name, (src, dst)) in enumerate(pairs.items())
    }
    loads["ids"].start()
    loads["lens"].start()

    barrier = pltpu.get_barrier_semaphore()

    def greet_table(i):
        pl.semaphore_signal(barrier, inc=1, device_id=(table_peer(i + 1), s), device_id_type=MESH)

    def greet_sample(i):
        pl.semaphore_signal(barrier, inc=1, device_id=(t, sample_peer(i + 1)), device_id_type=MESH)

    each(tables - 1, greet_table)
    each(samples - 1, greet_sample)

    for name, load in loads.items():
        if name not in ("ids", "lens"):
            load.start()

    def arrived(*names):
        for name in names:
            loads[name].wait()

    arrived("ids", "lens")
    slot_iota = lax.broadcasted_iota(jnp.int32, (tables, slots), 1)
    pieces = []
    for u in range(users):
        pieces.append(jnp.where(slot_iota < lens_ref[:, u : u + 1], ids_ref[u], -1))
    packed = jnp.concatenate(pieces, axis=1)
    for c in range(users * slots // LANES):
        msg[:, c, :] = packed[:, c * LANES : (c + 1) * LANES]
    for c in range(users * slots // LANES, chunks):
        msg[:, c, :] = jnp.full((tables, LANES), -1, jnp.int32)

    pl.semaphore_wait(barrier, tables - 1 + samples - 1)

    def ids_copy(dst_table, owner, src_table):
        return pltpu.make_async_remote_copy(
            src_ref=msg.at[src_table],
            dst_ref=got.at[owner],
            send_sem=ids_ssem.at[src_table],
            recv_sem=ids_rsem.at[owner],
            device_id=(dst_table, s),
            device_id_type=MESH,
        )

    def send_ids(i):
        peer = table_peer(i + 1)
        ids_copy(peer, t, peer).start()

    each(tables - 1, send_ids)
    got[t] = msg[t]

    arrived("imp", "label", "gain", "ws")
    imp_row = imp_ref[...].astype(F32)
    imp_col = to_column(imp_row, LANES)[:, :1]
    picks = jnp.where(
        imp_col == lax.broadcasted_iota(jnp.int32, (imps, group), 1).astype(F32), 1.0, 0.0
    ).astype(BF16)
    picks_t = jnp.where(
        imp_ref[...] == lax.broadcasted_iota(jnp.int32, (group, imps), 0), 1.0, 0.0
    ).astype(BF16)
    label_col = to_column(label_ref[...].astype(F32), LANES)[:, :1]
    v_row = gain_ref[...] * ws_ref[...]
    v_centred = v_row - jnp.mean(v_row, axis=1, keepdims=True)

    position = (
        lax.broadcasted_iota(jnp.int32, (chunks, LANES), 0) * LANES
        + lax.broadcasted_iota(jnp.int32, (chunks, LANES), 1)
    )
    user_of = jnp.zeros((chunks, LANES), jnp.int32)
    for u in range(1, users):
        user_of = user_of + jnp.where(position >= u * slots, 1, 0)
    user_of = jnp.where(user_of >= users // 2, user_of - users // 2, user_of)
    hi_iota = lax.broadcasted_iota(jnp.int32, (n_hi * users // 2, LANES), 0).astype(F32).astype(BF16)
    lo_iota = hi_iota[:LANES]
    one, zero = jnp.ones((), BF16), jnp.zeros((), BF16)
    used = users * slots // LANES

    def count_source(i):
        source = lax.rem(t + tables - i, tables)
        if isinstance(i, int):
            if i > 0:
                ids_copy(t, source, t).wait_recv()
        else:

            @pl.when(i > 0)
            def _():
                ids_copy(t, source, t).wait_recv()

        ids = got[source]
        hi_key = jnp.where(ids >= 0, (ids >> 7) * (users // 2) + user_of, -1).astype(F32).astype(BF16)
        lo_key = (ids & (LANES - 1)).astype(F32).astype(BF16)
        hi_hot, lo_hot = [], []
        for c in range(used):
            hi_hot.append(jnp.where(hi_key[c : c + 1, :] == hi_iota, one, zero))
            lo_hot.append(jnp.where(lo_key[c : c + 1, :] == lo_iota, one, zero))
        few, cut = users // 2, used // 2
        top, bottom = [
            dot_nt(
                jnp.concatenate(hi_hot[k : k + cut], axis=1),
                jnp.concatenate(lo_hot[k : k + cut], axis=1),
            )
            for k in (0, cut)
        ]
        rows = pl.ds(pl.multiple_of(i * users, users), users)
        for h in range(n_hi):
            own = slice(h * few, (h + 1) * few)
            both = jnp.concatenate([top[own], bottom[own]], axis=0)
            counts[rows, h * LANES : (h + 1) * LANES] = both.astype(BF16)

    def part_copy(dst_table, owner, slot):
        return pltpu.make_async_remote_copy(
            src_ref=part_send.at[slot],
            dst_ref=part_recv.at[owner],
            send_sem=part_ssem.at[slot],
            recv_sem=part_rsem.at[owner],
            device_id=(dst_table, s),
            device_id_type=MESH,
        )

    arrived("table")
    per_step = min(tables, 4)

    def pool_step(k):
        for j in range(per_step):
            count_source(k * per_step + j)
        rows = per_step * users
        part = dot_nn(counts[pl.ds(k * rows, rows), :], table_v[...]).astype(BF16)
        part_send[pl.ds(k * per_step, per_step)] = part.reshape(per_step, users, width)
        for j in range(per_step):
            i = k * per_step + j
            if isinstance(i, int):
                if i > 0:
                    part_copy(lax.rem(t + tables - i, tables), t, i).start()
            else:

                @pl.when(i > 0)
                def _():
                    part_copy(lax.rem(t + tables - i, tables), t, i).start()

    each(tables // per_step, pool_step)
    part_recv[t] = part_send[0]

    arrived("item", "wh", "wc", "bh", "bc")
    items = item_v[...]
    half = width
    pre_item = dot_nn(items, wh_v[half:, :]) + bh_ref[...]
    cross_item = dot_nn(items, wc_v[half:, :]) + (bc_ref[...] + 1.0)

    def take_part(i):
        source = lax.rem(t + tables - 1 - i, tables)
        part_copy(t, source, 0).wait_recv()

    each(tables - 1, take_part)
    pooled = jnp.sum(part_recv[...].astype(F32), axis=0) * scale
    pooled = pooled.astype(BF16)
    pool_all[s] = pooled

    def pool_copy(dst_sample, owner, sem):
        return pltpu.make_async_remote_copy(
            src_ref=pool_all.at[owner],
            dst_ref=pool_all.at[owner],
            send_sem=pool_ssem.at[sem],
            recv_sem=pool_rsem.at[owner],
            device_id=(t, dst_sample),
            device_id_type=MESH,
        )

    def send_pool(i):
        peer = sample_peer(i + 1)
        pool_copy(peer, s, peer).start()

    each(samples - 1, send_pool)
    stores = [pltpu.make_async_copy(pool_all.at[s], pooled_out, store_sem.at[0])]
    stores[0].start()
    arrived("wb")
    wb_t[...] = jnp.transpose(wb_v[...])
    wh_t[...] = jnp.transpose(wh_v[:half, :])
    wc_t[...] = jnp.transpose(wc_v[:half, :])

    def take_pool(i):
        source = lax.rem(s + samples - 1 - i, samples)
        pool_copy(s, source, s).wait_recv()

    each(samples - 1, take_pool)
    user_feat = dot_nn(picks, pool_all[...].reshape(group, width)).astype(BF16)

    pre_all = dot_nn(user_feat, wh_v[:half, :])
    cross_all = dot_nn(user_feat, wc_v[:half, :])
    columns = 2 * width
    lifted_all = jnp.concatenate([user_feat, items], axis=1)

    def activate(pre, pre_add):
        pre = pre + pre_add
        pre_sq = pre * pre
        tanh = jnp.tanh(pre * (GELU_A + (GELU_A * GELU_B) * pre_sq))
        gate = 0.5 + 0.5 * tanh
        rise = (0.5 * GELU_A) + (1.5 * GELU_A * GELU_B) * pre_sq
        slope = gate + pre * (1.0 - tanh * tanh) * rise
        return (pre * gate).astype(BF16), slope

    hidden, slope_all = by_rows(activate, pre_all, pre_item)
    back = dot_nn(hidden, wb_v[...])

    def score_rows(back, cross, cross_add, lifted, label):
        lifted = lifted.astype(F32)
        cross = cross + cross_add
        summed = back + lifted * cross
        row_mean = jnp.sum(summed, axis=1, keepdims=True) * (1.0 / columns)
        centred = summed - row_mean
        row_var = jnp.sum(centred * centred, axis=1, keepdims=True) * (1.0 / columns)
        raw_score = jnp.sum(centred * v_row, axis=1, keepdims=True)
        rstd = lax.rsqrt(row_var + 1e-05)
        score = raw_score * rstd
        pull = (jax.nn.sigmoid(score) - label) * rstd
        d_sum = pull * v_centred - centred * (pull * rstd * score * (1.0 / columns))
        return score, d_sum.astype(BF16), (d_sum * lifted).astype(BF16), d_sum * cross

    score, d_sum, d_cross, d_lift = by_rows(
        score_rows, back, cross_all, cross_item, lifted_all, label_col
    )
    d_hidden = dot_nn(d_sum, wb_t[...])
    (d_pre,) = by_rows(
        lambda d, slope: ((d.astype(BF16).astype(F32) * slope).astype(BF16),), d_hidden, slope_all
    )

    user_part = (
        d_lift[:, :half] + dot_nn(d_pre, wh_t[...]) + dot_nn(d_cross, wc_t[...])
    )
    per_user = dot_nn(picks_t, user_part.astype(BF16))
    grad_send[...] = per_user.astype(BF16).reshape(samples, users, width)

    def grad_copy(dst_sample, owner, src_sample):
        return pltpu.make_async_remote_copy(
            src_ref=grad_send.at[src_sample],
            dst_ref=grad_recv.at[owner],
            send_sem=grad_ssem.at[src_sample],
            recv_sem=grad_rsem.at[owner],
            device_id=(t, dst_sample),
            device_id_type=MESH,
        )

    def send_grad(i):
        peer = sample_peer(i + 1)
        grad_copy(peer, s, peer).start()

    each(samples - 1, send_grad)
    grad_recv[s] = grad_send[s]

    igrad_v[...] = (
        d_lift[:, half:] + dot_nt(d_pre, wh_v[half:, :]) + dot_nt(d_cross, wc_v[half:, :])
    )
    stores.append(pltpu.make_async_copy(igrad_v, igrad_out, store_sem.at[1]))
    stores[1].start()
    scores_v[...] = jnp.transpose(jnp.broadcast_to(score, (imps, LANES)))[:1, :]
    stores.append(pltpu.make_async_copy(scores_v, scores_out, store_sem.at[2]))
    stores[2].start()

    def take_grad(i):
        source = lax.rem(s + samples - 1 - i, samples)
        grad_copy(s, source, s).wait_recv()

    each(samples - 1, take_grad)
    ugrad_v[...] = jnp.sum(grad_recv[...].astype(F32), axis=0)
    stores.append(pltpu.make_async_copy(ugrad_v, ugrad_out, store_sem.at[3]))
    stores[3].start()

    def sent_table(i):
        peer = table_peer(i + 1)
        ids_copy(peer, t, peer).wait_send()
        part_copy(peer, t, i + 1).wait_send()

    def sent_sample(i):
        peer = sample_peer(i + 1)
        pool_copy(peer, s, peer).wait_send()
        grad_copy(peer, s, peer).wait_send()

    each(tables - 1, sent_table)
    each(samples - 1, sent_sample)
    for store in stores:
        store.wait()


def write_out(*refs):
    *arrays, sems = refs
    count = len(arrays) // 3
    sources, targets, held = arrays[:count], arrays[count : 2 * count], arrays[2 * count :]
    loads = [pltpu.make_async_copy(sources[i], held[i], sems.at[0, i]) for i in range(count)]
    stores = [pltpu.make_async_copy(held[i], targets[i], sems.at[1, i]) for i in range(count)]
    for load in loads[::-1]:
        load.start()
    for load, store in zip(loads, stores):
        load.wait()
        store.start()
    for store in stores:
        store.wait()


def body(tables, samples, *args):
    (
        hist_ids,
        hist_lens,
        table_rows,
        imp_user,
        item_rows,
        labels,
        w_hidden,
        b_hidden,
        w_back,
        w_cross,
        b_cross,
        norm_gain,
        w_score,
    ) = args
    users, _, slots = hist_ids.shape
    rows, width = table_rows.shape
    imps = item_rows.shape[0]
    history = slots * tables * 2 // 3
    assert (users * slots) % (2 * LANES) == 0 and rows % LANES == 0 and users % 16 == 0
    chunks = -(-(users * slots // LANES) // 8) * 8
    hbm = pl.BlockSpec(memory_space=pltpu.HBM)
    dma = pltpu.SemaphoreType.DMA

    def rowed(a):
        return a.reshape(1, -1)

    operands = (
        hist_ids,
        hist_lens.T,
        table_rows,
        rowed(imp_user),
        item_rows,
        rowed(labels),
        w_hidden,
        rowed(b_hidden),
        w_back,
        w_cross,
        rowed(b_cross),
        rowed(norm_gain),
        rowed(w_score),
    )
    shapes = (
        jax.ShapeDtypeStruct((users, width), BF16),
        jax.ShapeDtypeStruct((1, imps), F32),
        jax.ShapeDtypeStruct((users, width), F32),
        jax.ShapeDtypeStruct((imps, width), F32),
    )
    results = pl.pallas_call(
        functools.partial(kernel, float(history) ** (-0.5)),
        out_shape=shapes,
        in_specs=[hbm] * len(operands),
        out_specs=(hbm,) * len(shapes),
        scratch_shapes=[
            *[pltpu.VMEM(a.shape, a.dtype) for a in operands],
            pltpu.VMEM((tables, chunks, LANES), jnp.int32),
            pltpu.VMEM((tables, chunks, LANES), jnp.int32),
            pltpu.VMEM((tables * users, rows), BF16),
            pltpu.VMEM((tables, users, width), BF16),
            pltpu.VMEM((tables, users, width), BF16),
            pltpu.VMEM((samples, users, width), BF16),
            pltpu.VMEM((samples, users, width), BF16),
            pltpu.VMEM((samples, users, width), BF16),
            pltpu.VMEM((imps, width), F32),
            pltpu.VMEM((1, imps), F32),
            pltpu.VMEM((users, width), F32),
            pltpu.VMEM(w_back.shape[::-1], BF16),
            pltpu.VMEM((w_hidden.shape[1], width), BF16),
            pltpu.VMEM((w_cross.shape[1], width), BF16),
            dma((len(operands),)),
            dma((len(shapes),)),
            dma((tables,)),
            dma((tables,)),
            dma((tables,)),
            dma((tables,)),
            dma((samples,)),
            dma((samples,)),
            dma((samples,)),
            dma((samples,)),
        ],
        compiler_params=pltpu.CompilerParams(
            collective_id=0, has_side_effects=True, vmem_limit_bytes=VMEM_GRANT
        ),
        cost_estimate=pl.CostEstimate(
            flops=1_500_000_000, bytes_accessed=4_000_000, transcendentals=200_000
        ),
    )(*operands)
    pooled, scores, user_grad, item_grad = pl.pallas_call(
        write_out,
        out_shape=shapes,
        in_specs=[hbm] * len(shapes),
        out_specs=(hbm,) * len(shapes),
        scratch_shapes=[*[pltpu.VMEM(a.shape, a.dtype) for a in shapes], dma((2, len(shapes)))],
        compiler_params=pltpu.CompilerParams(vmem_limit_bytes=VMEM_GRANT),
    )(*results)
    return pooled, scores.reshape(imps), user_grad, item_grad


def solution(mesh):
    in_specs = (
        P(("table", "sample"), None, None),
        P(("table", "sample"), None),
        P("table", None),
        P(("table", "sample")),
        P(("table", "sample"), None),
        P(("table", "sample")),
        P(),
        P(),
        P(),
        P(),
        P(),
        P(),
        P(),
    )
    out_specs = (
        P(("table", "sample"), None),
        P(("table", "sample")),
        P(("table", "sample"), None),
        P(("table", "sample"), None),
    )
    step = functools.partial(body, mesh.shape["table"], mesh.shape["sample"])
    return jax.shard_map(step, mesh=mesh, in_specs=in_specs, out_specs=out_specs, check_vma=False)
```
